256 devices in a mesh: dp: 8 (over x, core), row: 8 (over z), col: 4 (over y).
Axes of the slice: x: 4, y: 4, z: 8, core: 2. Of those that a mesh axis runs over, the one named last changes fastest.
Arguments:
- calib: bfloat16 [4096, 8192], P('dp', 'col'), as said below
- weight: bfloat16 [26624, 8192], P(('dp', 'row'), 'col'), may hold values from -0.0625 to 0.0625
- sketch: bfloat16 [8192, 512], P('col', 'row'), may hold values from -6 to 6
Outputs:
- panels: float32 [26624, 512], P(('dp', 'row'))
- projections: float32 [512, 8192], P(('dp', 'row'), 'col')
The draws below stay inside these ranges and needn't reach their ends.
Inputs may be any that keep to these rules, and one draw needn't show every extreme that they name: `calib`: each feature and each token has its own scale.
All inputs are finite; a program needn't handle non-finite values.
Results may differ from the reference program's by a relative error of at most 0.0062.
Values may be sent and summed in bfloat16 or wider, within the bound.
No kernel may reach another device: no remote copies, remote signals or barrier semaphores. Data moves between devices by JAX's collectives and lax.ppermute only.
A program may use at most 128 MiB of HBM per device.

```python
import math
import jax
import jax.numpy as jnp
from jax import lax

D = 8192
FF = 26624
R = 512
WB = 512
TOKENS = 4096


def draw_calib(key, part):
    key = jax.random.fold_in(key, 11)
    key_feat, key_base = jax.random.split(key, 2)
    feat = jnp.exp(jax.random.uniform(key_feat, (D,), jnp.float32, 0.0, math.log(10.0)))
    ramp_feat = jnp.sqrt(1.0 + 2.0 * jnp.arange(D, dtype=jnp.float32) / (D - 1))
    ramp_tok = jnp.sqrt(1.0 + 2.0 * jnp.arange(TOKENS, dtype=jnp.float32) / (TOKENS - 1))
    base = jax.random.normal(key_base, (TOKENS, D), jnp.float32)
    values = 0.5 * base * feat[None, :] * ramp_feat[None, :] * ramp_tok[:, None]
    return values.astype(jnp.bfloat16)


def shard_levels(stream_key, extent, cuts, least, high):
    loudness = 1.0
    for dim, blocks in cuts:
        draws = jax.random.uniform(jax.random.fold_in(jax.random.fold_in(stream_key, 6), dim), (blocks,), jnp.float32, least / len(cuts), high / len(cuts))
        loudness = loudness * jnp.repeat(jnp.exp(draws), extent[dim] // blocks).reshape((-1,) + (1,) * (len(extent) - 1 - dim))
    return loudness


def centred(key, shape, spread, reach, cuts=(), kind=jnp.bfloat16):
    result = jax.random.normal(key, shape, jnp.float32) * spread
    if len(cuts) > 0:
        result = shard_levels(key, shape, cuts, -0.22, 0.18) * result
    return jnp.clip(result, min=-reach, max=reach).astype(kind)


def setup_inputs(seed: int = 0) -> dict:
    arg_keys = jax.random.split(jax.random.key(seed), 4)
    calib = draw_calib(jax.random.fold_in(arg_keys[3], 71), 0)
    weight = centred(arg_keys[1], (FF, D), D ** -0.5, 0.0625, ((0, 64), (1, 4)))
    sketch = centred(arg_keys[2], (D, R), 1.0, 6.0, ((0, 4), (1, 8)))
    return dict(calib=calib, weight=weight, sketch=sketch)


damping_ratio = 0.5

def reference(calib, weight, sketch):
    tokens = calib.shape[0]
    width = calib.shape[1]
    hidden = weight.shape[0]
    total = jnp.sum(jnp.square(calib.astype(jnp.float32)))
    lam = damping_ratio * total / (tokens * width)
    factors = []
    mixed_parts = []
    for block in range(width // WB):
        cols = calib[:, block * WB:(block + 1) * WB]
        gram = jnp.dot(cols.T.astype(jnp.float32), cols.astype(jnp.float32), preferred_element_type=jnp.float32) / tokens
        gram = gram + lam * jnp.eye(WB, dtype=jnp.float32)
        factor = jnp.linalg.cholesky(gram).astype(jnp.bfloat16)
        factors.append(factor)
        rows = sketch[block * WB:(block + 1) * WB, :]
        mixed_parts.append(jnp.dot(factor.astype(jnp.float32), rows.astype(jnp.float32), preferred_element_type=jnp.float32).astype(jnp.bfloat16))
    mixed = jnp.concatenate(mixed_parts, axis=0)
    ysum = jnp.dot(weight.astype(jnp.float32), mixed.astype(jnp.float32), preferred_element_type=jnp.float32)
    cross = jnp.dot(ysum.T, ysum, precision=lax.Precision.HIGHEST) / hidden
    rfac = jnp.linalg.cholesky(cross)
    panels = jax.scipy.linalg.solve_triangular(rfac, ysum.T, lower=True).T
    pb = panels.astype(jnp.bfloat16)
    moments = jnp.dot(pb.T.astype(jnp.float32), weight.astype(jnp.float32), preferred_element_type=jnp.float32)
    outs = []
    for block in range(width // WB):
        part = moments[:, block * WB:(block + 1) * WB]
        outs.append(jnp.dot(part, factors[block].astype(jnp.float32), precision=lax.Precision.HIGHEST))
    projections = jnp.concatenate(outs, axis=1) / math.sqrt(hidden)
    return (panels, projections)
```

```python
import math

import jax
import jax.numpy as jnp
from jax import lax
from jax.experimental import pallas as pl
from jax.experimental.pallas import tpu as pltpu
from jax.sharding import PartitionSpec as P

WB = 512
NB = 128
damping_ratio = 0.5
f32 = jnp.float32
bf16 = jnp.bfloat16
HI = lax.Precision.HIGHEST
PAIRS = [(i, j) for i in range(4) for j in range(i, 4)]
NP = len(PAIRS)
HALF = NP // 2


def tn(a, b, precision=None):
    return lax.dot_general(
        a, b, (((0,), (0,)), ((), ())), preferred_element_type=f32, precision=precision
    )


def nt(a, b, precision=None):
    return lax.dot_general(
        a, b, (((1,), (1,)), ((), ())), preferred_element_type=f32, precision=precision
    )


def nn(a, b, precision=None):
    return jnp.dot(a, b, preferred_element_type=f32, precision=precision)


def call(kernel, out_shape, n_smem, n_vmem, scratch=(), name=None):
    one = not isinstance(out_shape, (tuple, list))
    return pl.pallas_call(
        kernel,
        out_shape=out_shape,
        in_specs=[pl.BlockSpec(memory_space=pltpu.SMEM)] * n_smem
        + [pl.BlockSpec(memory_space=pltpu.VMEM)] * n_vmem,
        out_specs=pl.BlockSpec(memory_space=pltpu.VMEM)
        if one
        else tuple(pl.BlockSpec(memory_space=pltpu.VMEM) for _ in out_shape),
        scratch_shapes=list(scratch),
        compiler_params=pltpu.CompilerParams(vmem_limit_bytes=40 * 2**20),
        name=name,
    )


def shape(s, d=f32):
    return jax.ShapeDtypeStruct(s, d)


def sub(x, j):
    return jnp.broadcast_to(x[j : j + 1, :], (8, NB))


def lane(x, c):
    return jnp.broadcast_to(x[:, c : c + 1], (8, NB))


def diag_factor(rows):
    row = lax.broadcasted_iota(jnp.int32, (8, NB), 0)
    col = lax.broadcasted_iota(jnp.int32, (8, NB), 1)
    upper = list(rows)
    inv = [jnp.where(col == row + 8 * g, 1.0, 0.0).astype(f32) for g in range(16)]
    for g in range(16):
        c = [lane(upper[g], 8 * g + j) for j in range(8)]
        v, z = upper[g], inv[g]
        us, zs, ss, q = [], [], [], {}
        for j in range(8):
            s = lax.rsqrt(sub(c[j], j))
            u = sub(v, j) * s
            w = sub(z, j) * s
            m = jnp.where(row > j, c[j] * s, 0.0)
            for k in range(j + 1, 8):
                q[j, k] = sub(c[k], j) * s
                c[k] = c[k] - m * q[j, k]
            v = jnp.where(row == j, u, v - m * u)
            z = jnp.where(row == j, w, z - m * w)
            us.append(u)
            zs.append(w)
            ss.append(s)
        upper[g] = jnp.where(col >= row + 8 * g, v, 0.0)
        inv[g] = z
        for h in range(g + 1, 16):
            low = []
            for j in range(8):
                t = lane(upper[h], 8 * g + j)
                for k in range(j):
                    t = t - low[k] * q[k, j]
                low.append(t * ss[j])
            a, b = low[0] * us[0], low[0] * zs[0]
            for j in range(1, 8):
                a = a + low[j] * us[j]
                b = b + low[j] * zs[j]
            upper[h] = upper[h] - a
            inv[h] = inv[h] - b
    return upper, inv


def blk(i):
    return slice(NB * i, NB * i + NB)


def factor_blocks(a_ref, u_ref, d_ref, e_ref=None):
    for k in range(4):
        upper, inv = diag_factor([a_ref[NB * k + 8 * g : NB * k + 8 * g + 8, blk(k)] for g in range(16)])
        for g in range(16):
            u_ref[NB * k + 8 * g : NB * k + 8 * g + 8, blk(k)] = upper[g]
            d_ref[8 * g : 8 * g + 8, :] = inv[g]
        dinv = d_ref[...]
        for j in range(k + 1, 4):
            u_ref[blk(k), blk(j)] = nn(dinv, a_ref[blk(k), blk(j)], HI)
        for i in range(k + 1, 4):
            a_ref[blk(i), NB * i :] -= tn(u_ref[blk(k), blk(i)], u_ref[blk(k), NB * i :], HI)
        if e_ref is not None:
            if k:
                e_ref[blk(k), : NB * k] = nn(dinv, e_ref[blk(k), : NB * k], HI)
            e_ref[blk(k), blk(k)] = dinv
            for i in range(k + 1, 4):
                e_ref[blk(i), : NB * (k + 1)] -= tn(u_ref[blk(k), blk(i)], e_ref[blk(k), : NB * (k + 1)], HI)


def gram_kernel(ids, c_ref, o_ref, g_ref):
    r = ids[2]
    row = lax.broadcasted_iota(jnp.int32, (8, NB), 0)
    col = lax.broadcasted_iota(jnp.int32, (8, NB), 1)
    acc = jnp.zeros((8, NB), f32)
    for b in range(4):
        part = c_ref[:, WB * b : WB * b + WB]
        g_ref[...] = tn(part, part)
        for i in range(4):
            for g in range(16):
                tile = g_ref[NB * i + 8 * g : NB * i + 8 * g + 8, blk(i)]
                acc = acc + jnp.where(col == row + 8 * g, tile, 0.0)
        for half in range(2):
            for p, (i, j) in enumerate(PAIRS):
                start = pl.multiple_of(NB * i + 16 * r + 8 * half, 8)
                o_ref[2 * b + half, p] = g_ref[pl.ds(start, 8), blk(j)]
    for d in range(8):
        o_ref[d, NP] = acc


def chol_kernel(scale, lam_scale, ids, own_ref, oth_ref, s0, s1, s2, s3, o_ref, h_ref, a_ref, u_ref, d_ref):
    k = ids[1]
    total = jnp.sum(s0[...] + s1[...] + s2[...] + s3[...], keepdims=True)
    lam = jnp.broadcast_to(total * lam_scale, (8, NB))
    row = lax.broadcasted_iota(jnp.int32, (8, NB), 0)
    col = lax.broadcasted_iota(jnp.int32, (8, NB), 1)
    for half in range(2):
        side = lax.rem(k + half, 2)
        ref = own_ref if half == 0 else oth_ref
        for r in range(8):
            for p, (i, j) in enumerate(PAIRS):
                start = pl.multiple_of(NB * i + 16 * r + 8 * side, 8)
                tile = ref[r, p] * scale
                if i == j:
                    tile = tile + jnp.where(col == row + (16 * r + 8 * side), lam, 0.0)
                a_ref[pl.ds(start, 8), blk(j)] = tile
    factor_blocks(a_ref, u_ref, d_ref)
    for p, (i, j) in enumerate(PAIRS):
        o_ref[p] = u_ref[blk(i), blk(j)].astype(bf16)
    h_ref[...] = o_ref[pl.ds(HALF * k, HALF)]


def mixed_kernel(ids, own_ref, r1, r2, r3, t1, t2, t3, sk_ref, w_ref, y_ref, f_ref, full_ref):
    x, k = ids[0], ids[1]
    full_ref[...] = jnp.zeros((WB, WB), bf16)
    f_ref[0] = own_ref[...]
    for s, (a, b) in enumerate(((r1, t1), (r2, t2), (r3, t3))):
        f_ref[s + 1, pl.ds(HALF * k, HALF)] = a[...]
        f_ref[s + 1, pl.ds(HALF * (1 - k), HALF)] = b[...]
    for s in range(4):
        b = lax.rem(x - s + 4, 4)
        for p, (i, j) in enumerate(PAIRS):
            full_ref[blk(i), blk(j)] = f_ref[s, p]
        cols = pl.ds(pl.multiple_of(WB * b, WB), WB)
        mixed = tn(full_ref[...], sk_ref[cols, :]).astype(bf16)
        y = nn(w_ref[:, cols], mixed)
        if s == 0:
            y_ref[...] = y
        else:
            y_ref[...] += y


def cross_kernel(ids, y_ref, own_ref, oth_ref, ys_ref):
    k = ids[1]
    y = (y_ref[0] + y_ref[1]) + (y_ref[2] + y_ref[3])
    ys_ref[...] = y
    for side in range(2):
        blocks = [nn_t(y[:, blk(i)], y[:, blk(j)]) for i, j in PAIRS[HALF * side : HALF * side + HALF]]

        def put(ref, blocks=blocks):
            for q, c in enumerate(blocks):
                for g in range(16):
                    ref[g, q] = c[8 * g : 8 * g + 8, :]

        pl.when(k == side)(lambda: put(own_ref))
        pl.when(k != side)(lambda: put(oth_ref))


def nn_t(a, b):
    return tn(a, b, HI)


def chol2_kernel(scale, ids, own_ref, oth_ref, o_ref, a_ref, u_ref, d_ref):
    k = ids[1]

    def put(first, second):
        for side, ref in enumerate((first, second)):
            for q, (i, j) in enumerate(PAIRS[HALF * side : HALF * side + HALF]):
                for g in range(16):
                    a_ref[NB * i + 8 * g : NB * i + 8 * g + 8, blk(j)] = ref[g, q] * scale

    pl.when(k == 0)(lambda: put(own_ref, oth_ref))
    pl.when(k != 0)(lambda: put(oth_ref, own_ref))
    o_ref[...] = jnp.zeros((WB, WB), f32)
    factor_blocks(a_ref, u_ref, d_ref, o_ref)


def moment_kernel(ids, y0, y1, y2, y3, w_ref, own_ref, oth_ref, y_ref, yb_ref):
    x, k, c = ids[0], ids[1], ids[3]
    n = y0.shape[0]
    for s, ref in enumerate((y0, y1, y2, y3)):
        start = pl.multiple_of(lax.rem(c - s + 4, 4) * n, 8)
        y_ref[pl.ds(start, n), :] = ref[...]
    yb_ref[...] = y_ref[...].astype(bf16)
    for s in range(4):
        to = lax.rem(x + s, 4)
        cols = pl.ds(pl.multiple_of(lax.rem(to, 2) * 1024, 1024), 1024)
        for half in range(2):
            side = lax.rem(k + half, 2)
            kr = 2 * side + lax.div(to, 2)
            t = tn(yb_ref[:, pl.ds(pl.multiple_of(kr * NB, NB), NB)], w_ref[:, cols])
            for r in range(8):
                if half == 0:
                    own_ref[s, r] = t[:, blk(r)]
                else:
                    oth_ref[s, r] = t[:, blk(r)].astype(bf16)


def part_kernel(ids, inv_ref, s_ref, o_ref):
    x, k = ids[0], ids[1]
    kr = 2 * k + lax.div(x, 2)
    m = nn(inv_ref[:, pl.ds(pl.multiple_of(kr * NB, NB), NB)], s_ref[...], HI)
    o_ref[...] = m.reshape(64, 8, NB)


def panel_kernel(inv_ref, y_ref, o_ref):
    o_ref[...] = nt(y_ref[...], inv_ref[...], HI)


def final_kernel(scale, ids, m_ref, f_ref, o_ref, mom_ref, full_ref):
    x = ids[0]
    for cg in range(16):
        tile = None
        for kr in range(4):
            src = ((kr % 2) * 2 + cg // 8) * 16 + (kr // 2) * 8 + cg % 8
            tile = m_ref[src] if tile is None else tile + m_ref[src]
        mom_ref[:, blk(cg)] = tile * scale
    full_ref[...] = jnp.zeros((WB, WB), bf16)
    for s in range(4):
        b = lax.rem(x - s + 4, 4)
        for p, (i, j) in enumerate(PAIRS):
            full_ref[blk(i), blk(j)] = f_ref[s, p]
        cols = pl.ds(pl.multiple_of(WB * b, WB), WB)
        m = mom_ref[:, cols]
        hi = m.astype(bf16)
        rest = m - hi.astype(f32)
        mid = rest.astype(bf16)
        low = (rest - mid.astype(f32)).astype(bf16)
        full = full_ref[...]
        o_ref[:, cols] = nt(hi, full) + (nt(mid, full) + nt(low, full))


def shift(v, axis, s, n):
    return lax.ppermute(v, axis, [(i, (i + s) % n) for i in range(n)])


def everyone(v, axis, n):
    return lax.all_to_all(jnp.broadcast_to(v[None], (n,) + v.shape), axis, 0, 0, tiled=True)


def shards(calib, weight, sketch):
    tokens = calib.shape[0] * 8
    width = calib.shape[1] * 4
    hidden = weight.shape[0] * 64
    ids = jnp.stack([lax.axis_index(a) for a in ("x", "core", "row", "col")]).astype(jnp.int32)

    sketch_all = lax.all_gather(sketch, "row", axis=1, tiled=True)

    grams = call(gram_kernel, shape((8, NP + 1, 8, NB)), 1, 1, [pltpu.VMEM((WB, WB), f32)], "gram")(ids, calib)
    slab = jnp.sum(lax.all_to_all(grams, ("x", "core"), 0, 0, tiled=True), axis=0)
    trace = slab[NP]
    traces = [trace] + [shift(trace, "col", s, 4) for s in (1, 2, 3)]
    own = everyone(slab[:NP], "row", 8)
    oth = shift(own, "core", 1, 2)
    square = pltpu.VMEM((WB, WB), f32)
    diag = pltpu.VMEM((NB, NB), f32)

    def chol1(*refs):
        chol_kernel(1.0 / tokens, damping_ratio / (tokens * width), *refs)

    fac, fac_half = call(
        chol1, (shape((NP, NB, NB), bf16), shape((HALF, NB, NB), bf16)), 1, 6, [square, square, diag], "chol_gram"
    )(ids, own, oth, *traces)
    got = [shift(fac_half, "x", s, 4) for s in (1, 2, 3)]
    got_oth = [shift(v, "core", 1, 2) for v in got]
    ypart, factors = call(
        mixed_kernel,
        (shape((weight.shape[0], WB)), shape((4, NP, NB, NB), bf16)),
        1,
        9,
        [pltpu.VMEM((WB, WB), bf16)],
        "mixed",
    )(ids, fac, *got, *got_oth, sketch_all, weight)

    n = weight.shape[0] // 4
    ypieces = lax.all_to_all(ypart.reshape(4, n, WB), "col", 0, 0, tiled=True)
    tri = shape((16, HALF, 8, NB))
    cown, coth, ysum = call(cross_kernel, (tri, tri, shape((n, WB))), 1, 1, [], "cross")(ids, ypieces)
    ys = [ysum] + [shift(ysum, "col", s, 4) for s in (1, 2, 3)]
    half = cown + shift(coth, "core", 1, 2)
    piece = jnp.sum(lax.all_to_all(half, ("x", "col"), 0, 0, tiled=True), axis=0)
    piece = jnp.sum(everyone(piece, "row", 8), axis=0)
    half = everyone(piece, ("x", "col"), 16)
    coth = shift(half, "core", 1, 2)

    def chol2(*refs):
        chol2_kernel(1.0 / hidden, *refs)

    inv = call(chol2, shape((WB, WB)), 1, 2, [square, square, diag], "chol_cross")(ids, half, coth)

    town, toth, yfull = call(
        moment_kernel,
        (shape((4, 8, NB, NB)), shape((4, 8, NB, NB), bf16), shape((4 * n, WB))),
        1,
        5,
        [pltpu.VMEM((4 * n, WB), bf16)],
        "moments",
    )(ids, *ys, weight)
    t = town + shift(toth, "core", 1, 2).astype(f32)
    tile = t[0]
    for s in (1, 2, 3):
        tile = tile + shift(t[s].astype(bf16), "x", s, 4).astype(f32)
    tile = lax.psum_scatter(tile, "row", scatter_dimension=0, tiled=True)[0]

    parts = call(part_kernel, shape((64, 8, NB)), 1, 2, [], "project")(ids, inv, tile)
    parts = lax.all_to_all(parts, ("x", "core", "row"), 0, 0, tiled=True)

    def final(*refs):
        final_kernel(1.0 / math.sqrt(hidden), *refs)

    projections = call(
        final, shape((8, 4 * WB)), 1, 2, [pltpu.VMEM((8, 4 * WB), f32), pltpu.VMEM((WB, WB), bf16)], "final"
    )(ids, parts, factors)
    panels = call(panel_kernel, shape((4 * n, WB)), 0, 2, [], "panels")(inv, yfull)
    return (panels, projections)


def solution(mesh):
    fine = jax.sharding.Mesh(mesh.devices.reshape(4, 2, 8, 4), ("x", "core", "row", "col"))
    return jax.shard_map(
        shards,
        mesh=fine,
        in_specs=(P(("x", "core"), "col"), P(("x", "core", "row"), "col"), P("col", "row")),
        out_specs=(P(("x", "core", "row"), None), P(("x", "core", "row"), "col")),
        check_vma=False,
    )
```

```python
import math

import jax
import jax.numpy as jnp
from jax import lax
from jax.experimental import pallas as pl
from jax.experimental.pallas import tpu as pltpu
from jax.sharding import PartitionSpec as P

WB = 512
NB = 128
damping_ratio = 0.5
f32 = jnp.float32
bf16 = jnp.bfloat16
HI = lax.Precision.HIGHEST
PAIRS = [(i, j) for i in range(4) for j in range(i, 4)]
NP = len(PAIRS)
HALF = NP // 2


def tn(a, b, precision=None):
    return lax.dot_general(
        a, b, (((0,), (0,)), ((), ())), preferred_element_type=f32, precision=precision
    )


def nt(a, b, precision=None):
    return lax.dot_general(
        a, b, (((1,), (1,)), ((), ())), preferred_element_type=f32, precision=precision
    )


def nn(a, b, precision=None):
    return jnp.dot(a, b, preferred_element_type=f32, precision=precision)


SPACES = {"s": pltpu.SMEM, "v": pltpu.VMEM, "a": pl.ANY, "h": pltpu.HBM}


def call(kernel, out_shape, ins, outs, scratch=(), name=None):
    one = not isinstance(out_shape, (tuple, list))
    out_specs = tuple(pl.BlockSpec(memory_space=SPACES[c]) for c in outs)
    return pl.pallas_call(
        kernel,
        out_shape=out_shape,
        in_specs=[pl.BlockSpec(memory_space=SPACES[c]) for c in ins],
        out_specs=out_specs[0] if one else out_specs,
        scratch_shapes=list(scratch),
        compiler_params=pltpu.CompilerParams(vmem_limit_bytes=40 * 2**20),
        name=name,
    )


def shape(s, d=f32):
    return jax.ShapeDtypeStruct(s, d)


def sub(x, j):
    return jnp.broadcast_to(x[j : j + 1, :], (8, NB))


def lane(x, c):
    return jnp.broadcast_to(x[:, c : c + 1], (8, NB))


def diag_factor(rows):
    row = lax.broadcasted_iota(jnp.int32, (8, NB), 0)
    col = lax.broadcasted_iota(jnp.int32, (8, NB), 1)
    upper = list(rows)
    inv = [jnp.where(col == row + 8 * g, 1.0, 0.0).astype(f32) for g in range(16)]
    for g in range(16):
        c = [lane(upper[g], 8 * g + j) for j in range(8)]
        v, z = upper[g], inv[g]
        us, zs, ss, q = [], [], [], {}
        for j in range(8):
            s = lax.rsqrt(sub(c[j], j))
            u = sub(v, j) * s
            w = sub(z, j) * s
            m = jnp.where(row > j, c[j] * s, 0.0)
            for k in range(j + 1, 8):
                q[j, k] = sub(c[k], j) * s
                c[k] = c[k] - m * q[j, k]
            v = jnp.where(row == j, u, v - m * u)
            z = jnp.where(row == j, w, z - m * w)
            us.append(u)
            zs.append(w)
            ss.append(s)
        upper[g] = jnp.where(col >= row + 8 * g, v, 0.0)
        inv[g] = z
        for h in range(g + 1, 16):
            low = []
            for j in range(8):
                t = lane(upper[h], 8 * g + j)
                for k in range(j):
                    t = t - low[k] * q[k, j]
                low.append(t * ss[j])
            a, b = low[0] * us[0], low[0] * zs[0]
            for j in range(1, 8):
                a = a + low[j] * us[j]
                b = b + low[j] * zs[j]
            upper[h] = upper[h] - a
            inv[h] = inv[h] - b
    return upper, inv


def blk(i):
    return slice(NB * i, NB * i + NB)


def factor_blocks(a_ref, u_ref, d_ref, e_ref=None):
    for k in range(4):
        upper, inv = diag_factor([a_ref[NB * k + 8 * g : NB * k + 8 * g + 8, blk(k)] for g in range(16)])
        for g in range(16):
            u_ref[NB * k + 8 * g : NB * k + 8 * g + 8, blk(k)] = upper[g]
            d_ref[8 * g : 8 * g + 8, :] = inv[g]
        dinv = d_ref[...]
        for j in range(k + 1, 4):
            u_ref[blk(k), blk(j)] = nn(dinv, a_ref[blk(k), blk(j)], HI)
        for i in range(k + 1, 4):
            a_ref[blk(i), NB * i :] -= tn(u_ref[blk(k), blk(i)], u_ref[blk(k), NB * i :], HI)
        if e_ref is not None:
            if k:
                e_ref[blk(k), : NB * k] = nn(dinv, e_ref[blk(k), : NB * k], HI)
            e_ref[blk(k), blk(k)] = dinv
            for i in range(k + 1, 4):
                e_ref[blk(i), : NB * (k + 1)] -= tn(u_ref[blk(k), blk(i)], e_ref[blk(k), : NB * (k + 1)], HI)


def fetch(src, dst, sem):
    copy = pltpu.make_async_copy(src, dst, sem)
    copy.start()
    return copy


def gram_kernel(ids, c_hbm, o_ref, c_ref, g_ref, sems):
    r = ids[2]
    copies = [
        fetch(c_hbm.at[:, WB * b : WB * b + WB], c_ref.at[:, WB * b : WB * b + WB], sems.at[b]) for b in range(4)
    ]
    row = lax.broadcasted_iota(jnp.int32, (8, NB), 0)
    col = lax.broadcasted_iota(jnp.int32, (8, NB), 1)
    acc = jnp.zeros((8, NB), f32)
    for b in range(4):
        copies[b].wait()
        part = c_ref[:, WB * b : WB * b + WB]
        g_ref[...] = tn(part, part)
        for i in range(4):
            for g in range(16):
                tile = g_ref[NB * i + 8 * g : NB * i + 8 * g + 8, blk(i)]
                acc = acc + jnp.where(col == row + 8 * g, tile, 0.0)
        for half in range(2):
            for p, (i, j) in enumerate(PAIRS):
                start = pl.multiple_of(NB * i + 16 * r + 8 * half, 8)
                o_ref[2 * b + half, p] = g_ref[pl.ds(start, 8), blk(j)]
    for d in range(8):
        o_ref[d, NP] = acc


def chol_kernel(scale, lam_scale, ids, own_ref, oth_ref, s0, s1, s2, s3, o_ref, h_ref, a_ref, u_ref, d_ref):
    k = ids[1]
    total = jnp.sum(s0[...] + s1[...] + s2[...] + s3[...], keepdims=True)
    lam = jnp.broadcast_to(total * lam_scale, (8, NB))
    row = lax.broadcasted_iota(jnp.int32, (8, NB), 0)
    col = lax.broadcasted_iota(jnp.int32, (8, NB), 1)
    for half in range(2):
        side = lax.rem(k + half, 2)
        ref = own_ref if half == 0 else oth_ref
        for r in range(8):
            for p, (i, j) in enumerate(PAIRS):
                start = pl.multiple_of(NB * i + 16 * r + 8 * side, 8)
                tile = ref[r, p] * scale
                if i == j:
                    tile = tile + jnp.where(col == row + (16 * r + 8 * side), lam, 0.0)
                a_ref[pl.ds(start, 8), blk(j)] = tile
    factor_blocks(a_ref, u_ref, d_ref)
    for p, (i, j) in enumerate(PAIRS):
        o_ref[p] = u_ref[blk(i), blk(j)].astype(bf16)
    h_ref[...] = o_ref[pl.ds(HALF * k, HALF)]


def mixed_kernel(ids, own, r1, r2, r3, t1, t2, t3, sk_hbm, w_ref, y_ref, f_hbm, sk_ref, f_ref, sems):
    x, k = ids[0], ids[1]
    copies = [fetch(sk_hbm, sk_ref, sems.at[0])]
    for s, pieces in enumerate((((own, 0), (own, 1)), ((r1, 0), (t1, 1)), ((r2, 0), (t2, 1)), ((r3, 0), (t3, 1)))):
        for ref, other in pieces:
            side = lax.rem(k + other, 2)
            for q in range(HALF):
                (i0, j0), (i1, j1) = PAIRS[q], PAIRS[HALF + q]
                i = pl.multiple_of(NB * (i0 + side * (i1 - i0)), NB)
                j = pl.multiple_of(NB * (j0 + side * (j1 - j0)), NB)
                src = ref.at[HALF * side + q] if s == 0 else ref.at[q]
                n = 1 + s * NP + other * HALF + q
                copies.append(fetch(src, f_ref.at[s, pl.ds(i, NB), pl.ds(j, NB)], sems.at[n]))
    for s in range(4):
        for i in range(4):
            for j in range(i):
                f_ref[s, blk(i), blk(j)] = jnp.zeros((NB, NB), bf16)
    outs = []
    for s in range(4):
        for copy in copies[1 + s * NP : 1 + (s + 1) * NP]:
            copy.wait()
        outs.append(fetch(f_ref.at[s], f_hbm.at[s], sems.at[1 + 4 * NP + s]))
    copies[0].wait()
    total = None
    for s in range(4):
        cols = pl.ds(pl.multiple_of(WB * lax.rem(x - s + 4, 4), WB), WB)
        mixed = nn(sk_ref[:, cols], f_ref[s]).astype(bf16)
        y = nt(w_ref[:, cols], mixed)
        total = y if s == 0 else total + y
    n = y_ref.shape[1]
    for c in range(4):
        y_ref[c] = total[n * c : n * c + n, :].astype(y_ref.dtype)
    for copy in outs:
        copy.wait()


def cross_kernel(ids, y_ref, own_ref, oth_ref, ys_ref):
    k = ids[1]
    y0, y1, y2, y3 = (y_ref[c].astype(f32) for c in range(4))
    y = ((y0 + y1) + (y2 + y3)).astype(bf16)
    ys_ref[...] = y
    for side in range(2):
        blocks = [tn(y[:, blk(i)], y[:, blk(j)]) for i, j in PAIRS[HALF * side : HALF * side + HALF]]

        def put(ref, blocks=blocks):
            for q, c in enumerate(blocks):
                for g in range(16):
                    ref[g, q] = c[8 * g : 8 * g + 8, :]

        pl.when(k == side)(lambda: put(own_ref))
        pl.when(k != side)(lambda: put(oth_ref))


def chol2_kernel(scale, ids, own_ref, oth_ref, o_ref, a_ref, u_ref, d_ref):
    k = ids[1]

    def put(first, second):
        for side, ref in enumerate((first, second)):
            for q, (i, j) in enumerate(PAIRS[HALF * side : HALF * side + HALF]):
                for g in range(16):
                    a_ref[NB * i + 8 * g : NB * i + 8 * g + 8, blk(j)] = ref[g, q] * scale

    pl.when(k == 0)(lambda: put(own_ref, oth_ref))
    pl.when(k != 0)(lambda: put(oth_ref, own_ref))
    o_ref[...] = jnp.zeros((WB, WB), f32)
    factor_blocks(a_ref, u_ref, d_ref, o_ref)


def moment_tiles(ids, s, side, yb_ref, w_ref):
    to = lax.rem(ids[0] + s, 4)
    cols = pl.ds(pl.multiple_of(lax.rem(to, 2) * 1024, 1024), 1024)
    kr = 2 * side + lax.div(to, 2)
    t = tn(yb_ref[:, pl.ds(pl.multiple_of(kr * NB, NB), NB)], w_ref[:, cols])
    return [t[:, blk(r)] for r in range(8)]


def send_kernel(ids, y0, y1, y2, y3, w_ref, oth_ref, yb_ref, yf_ref):
    n = y0.shape[0]
    for s, ref in enumerate((y0, y1, y2, y3)):
        start = pl.multiple_of(lax.rem(ids[3] - s + 4, 4) * n, 8)
        yf_ref[pl.ds(start, n), :] = ref[...].astype(f32)
    yb_ref[...] = yf_ref[...].astype(bf16)
    for s in range(4):
        for r, t in enumerate(moment_tiles(ids, s, 1 - ids[1], yb_ref, w_ref)):
            oth_ref[s, r] = t.astype(bf16)


def keep_kernel(ids, yb_ref, w_ref, own_ref):
    for s in range(4):
        for r, t in enumerate(moment_tiles(ids, s, ids[1], yb_ref, w_ref)):
            own_ref[s, r] = t


def fold_kernel(own_ref, got_ref, t0, t1, t2, t3):
    for s, ref in enumerate((t0, t1, t2, t3)):
        ref[...] = (own_ref[s] + got_ref[s].astype(f32)).astype(ref.dtype)


def split(v):
    hi = v.astype(bf16)
    rest = v - hi.astype(f32)
    mid = rest.astype(bf16)
    return hi, mid, (rest - mid.astype(f32)).astype(bf16)


def part_kernel(ids, inv_ref, s_hbm, o_ref, s_ref, sem):
    fetch(s_hbm.at[0], s_ref, sem).wait()
    x, k = ids[0], ids[1]
    kr = 2 * k + lax.div(x, 2)
    m = nn(inv_ref[:, pl.ds(pl.multiple_of(kr * NB, NB), NB)], s_ref[...], HI)
    o_ref[...] = m.reshape(64, 8, NB)


def panel_kernel(inv_ref, y_ref, o_ref):
    y = y_ref[...]
    hi, mid, low = (nt(y, v) for v in split(inv_ref[...]))
    o_ref[...] = hi + (mid + low)


def final_kernel(scale, ids, m_ref, f_ref, o_ref, mom_ref):
    x = ids[0]
    for cg in range(16):
        tile = None
        for kr in range(4):
            src = ((kr % 2) * 2 + cg // 8) * 16 + (kr // 2) * 8 + cg % 8
            tile = m_ref[src] if tile is None else tile + m_ref[src]
        mom_ref[:, blk(cg)] = tile * scale
    for s in range(4):
        cols = pl.ds(pl.multiple_of(WB * lax.rem(x - s + 4, 4), WB), WB)
        terms = jnp.concatenate([v.astype(f32) for v in split(mom_ref[:, cols])], axis=0).astype(bf16)
        p = nt(terms, f_ref[s])
        o_ref[:, cols] = p[:8] + (p[8:16] + p[16:])


def shift(v, axis, s, n):
    return lax.ppermute(v, axis, [(i, (i + s) % n) for i in range(n)])


def everyone(v, axis, n):
    return lax.all_to_all(jnp.broadcast_to(v[None], (n,) + v.shape), axis, 0, 0, tiled=True)


def shards(calib, weight, sketch):
    tokens = calib.shape[0] * 8
    width = calib.shape[1] * 4
    hidden = weight.shape[0] * 64
    ids = jnp.stack([lax.axis_index(a) for a in ("x", "core", "row", "col")]).astype(jnp.int32)

    n = weight.shape[0] // 4
    square = pltpu.VMEM((WB, WB), f32)
    diag = pltpu.VMEM((NB, NB), f32)
    dmas = pltpu.SemaphoreType.DMA

    grams = call(
        gram_kernel,
        shape((8, NP + 1, 8, NB)),
        "sh",
        "v",
        [pltpu.VMEM(calib.shape, bf16), square, dmas((4,))],
        "gram",
    )(ids, calib)
    slab = jnp.sum(lax.all_to_all(grams, ("x", "core"), 0, 0, tiled=True), axis=0)
    trace = slab[NP]
    traces = [trace] + [shift(trace, "col", s, 4) for s in (1, 2, 3)]
    own = everyone(slab[:NP], "row", 8)
    own, *traces = lax.optimization_barrier([own] + traces)
    oth = shift(own, "core", 1, 2)
    turned, _ = lax.optimization_barrier((sketch.T, own))
    sk_all = lax.all_gather(turned, "row", axis=0, tiled=True)

    def chol1(*refs):
        chol_kernel(1.0 / tokens, damping_ratio / (tokens * width), *refs)

    fac, fac_half = call(
        chol1,
        (shape((NP, NB, NB), bf16), shape((HALF, NB, NB), bf16)),
        "svvvvvv",
        "vv",
        [square, square, diag],
        "chol_gram",
    )(ids, own, oth, *traces)
    got = [shift(fac_half, "x", s, 4) for s in (1, 2, 3)]
    got_oth = [shift(v, "core", 1, 2) for v in got]
    ypart, factors = call(
        mixed_kernel,
        (shape((4, n, WB), bf16), shape((4, WB, WB), bf16)),
        "saaaaaaahv",
        "vh",
        [pltpu.VMEM(sk_all.shape, bf16), pltpu.VMEM((4, WB, WB), bf16), dmas((1 + 4 * NP + 4,))],
        "mixed",
    )(ids, fac, *got, *got_oth, sk_all, weight)

    ypieces = lax.all_to_all(ypart, "col", 0, 0, tiled=True)
    tri = shape((16, HALF, 8, NB))
    cown, coth, ysum = call(cross_kernel, (tri, tri, shape((n, WB), bf16)), "sv", "vvv", [], "cross")(ids, ypieces)
    ys = [shift(ysum, "col", s, 4) for s in (1, 2, 3)]
    half = cown + shift(coth, "core", 1, 2)
    piece = jnp.sum(lax.all_to_all(half, ("x", "col"), 0, 0, tiled=True), axis=0)
    piece, *ys = lax.optimization_barrier([piece] + ys)

    tiles = (4, 8, NB, NB)
    toth, yb = call(
        send_kernel,
        (shape(tiles, bf16), shape((4 * n, WB), bf16)),
        "svvvvv",
        "vv",
        [pltpu.VMEM((4 * n, WB), f32)],
        "moments_send",
    )(ids, ysum, *ys, weight)
    town = call(keep_kernel, shape(tiles), "svv", "v", [], "moments_keep")(ids, yb, weight)
    row_tiles = tiles[1:]
    t = call(
        fold_kernel, (shape(row_tiles),) + (shape(row_tiles, bf16),) * 3, "vv", "vvvv", [], "moments_fold"
    )(town, shift(toth, "core", 1, 2))
    piece, *t = lax.optimization_barrier([piece] + list(t))
    got = [shift(t[s], "x", s, 4) for s in (1, 2, 3)]
    piece = jnp.sum(everyone(piece, "row", 8), axis=0)
    piece, *got = lax.optimization_barrier([piece] + got)
    tile = t[0]
    for v in got:
        tile = tile + v.astype(f32)
    piece, tile = lax.optimization_barrier((piece, tile))
    tile = lax.psum_scatter(tile, "row", scatter_dimension=0, tiled=True)
    half = everyone(piece, ("x", "col"), 16)
    coth = shift(half, "core", 1, 2)

    def chol2(*refs):
        chol2_kernel(1.0 / hidden, *refs)

    inv = call(chol2, shape((WB, WB)), "svv", "v", [square, square, diag], "chol_cross")(ids, half, coth)
    parts = call(part_kernel, shape((64, 8, NB)), "sva", "v", [pltpu.VMEM((NB, NB), f32), dmas], "project")(
        ids, inv, tile
    )
    parts = lax.all_to_all(parts, ("x", "core", "row"), 0, 0, tiled=True)

    def final(*refs):
        final_kernel(1.0 / math.sqrt(hidden), *refs)

    projections = call(final, shape((8, 4 * WB)), "svv", "v", [pltpu.VMEM((8, 4 * WB), f32)], "final")(
        ids, parts, factors
    )
    panels = call(panel_kernel, shape((4 * n, WB)), "vv", "v", [], "panels")(inv, yb)
    return (panels, projections)


def solution(mesh):
    fine = jax.sharding.Mesh(mesh.devices.reshape(4, 2, 8, 4), ("x", "core", "row", "col"))
    return jax.shard_map(
        shards,
        mesh=fine,
        in_specs=(P(("x", "core"), "col"), P(("x", "core", "row"), "col"), P("col", "row")),
        out_specs=(P(("x", "core", "row"), None), P(("x", "core", "row"), "col")),
        check_vma=False,
    )
```

```python
import math

import jax
import jax.numpy as jnp
from jax import lax
from jax.experimental import pallas as pl
from jax.experimental.pallas import tpu as pltpu
from jax.sharding import PartitionSpec as P

WB = 512
NB = 128
damping_ratio = 0.5
f32 = jnp.float32
bf16 = jnp.bfloat16
HI = lax.Precision.HIGHEST
PAIRS = [(i, j) for i in range(4) for j in range(i, 4)]
NP = len(PAIRS)
HALF = NP // 2


def tn(a, b, precision=None):
    return lax.dot_general(
        a, b, (((0,), (0,)), ((), ())), preferred_element_type=f32, precision=precision
    )


def nt(a, b, precision=None):
    return lax.dot_general(
        a, b, (((1,), (1,)), ((), ())), preferred_element_type=f32, precision=precision
    )


def nn(a, b, precision=None):
    return jnp.dot(a, b, preferred_element_type=f32, precision=precision)


SPACES = {"s": pltpu.SMEM, "v": pltpu.VMEM, "a": pl.ANY, "h": pltpu.HBM}


def call(kernel, out_shape, ins, outs, scratch=(), name=None, mib=16, cost=None):
    one = not isinstance(out_shape, (tuple, list))
    out_specs = tuple(pl.BlockSpec(memory_space=SPACES[c]) for c in outs)
    return pl.pallas_call(
        kernel,
        out_shape=out_shape,
        in_specs=[pl.BlockSpec(memory_space=SPACES[c]) for c in ins],
        out_specs=out_specs[0] if one else out_specs,
        scratch_shapes=list(scratch),
        compiler_params=pltpu.CompilerParams(vmem_limit_bytes=mib * 2**20),
        name=name,
        cost_estimate=cost,
    )


def shape(s, d=f32):
    return jax.ShapeDtypeStruct(s, d)


def sub(x, j):
    return jnp.broadcast_to(x[j : j + 1, :], (8, NB))


def lane(x, c):
    return jnp.broadcast_to(x[:, c : c + 1], (8, NB))


def tree(t):
    return ((t[0] + t[1]) + (t[2] + t[3])) + ((t[4] + t[5]) + (t[6] + t[7]))


def diag_factor(rows):
    row = lax.broadcasted_iota(jnp.int32, (8, NB), 0)
    col = lax.broadcasted_iota(jnp.int32, (8, NB), 1)
    mat = list(rows)
    upper, inv = [], []
    c = [lane(mat[0], j) for j in range(8)]
    for g in range(16):
        inside = (col >= 8 * g) & (col < 8 * g + 8)
        v = jnp.where(inside, jnp.where(col == row + 8 * g, 1.0, 0.0), mat[g])
        rs, q = [], {}
        root = jnp.zeros((8, NB), f32)
        recip = root
        for j in range(8):
            p = sub(c[j], j)
            r = 1.0 / p
            below = jnp.where(row > j, c[j], 0.0)
            for k in range(j + 1, 8):
                q[j, k] = sub(c[k], j)
                c[k] = c[k] - (below * q[j, k]) * r
            v = v - below * (sub(v, j) * r)
            root = jnp.where(row == j, lax.rsqrt(p), root)
            recip = jnp.where(row == j, r, recip)
            rs.append(r)
        scaled = v * root
        own = jnp.zeros((8, NB), f32)
        for k in range(8):
            own = jnp.where(col == 8 * g + k, c[k], own)
        own = jnp.where(col >= row + 8 * g, own * root, 0.0)
        upper.append(jnp.where(col >= 8 * g + 8, scaled, own))
        inv.append(jnp.where(col < 8 * g + 8, scaled, 0.0))
        if g == 15:
            break
        raw = [lane(mat[g + 1], 8 * g + 8 + k) for k in range(8)]
        first = [lane(mat[g + 1], 8 * g + k) for k in range(8)]
        low = []
        for j in range(8):
            t = first[j]
            for i in range(j):
                t = t - low[i] * (q[i, j] * rs[i])
            low.append(t)
        mult = [low[j] * rs[j] for j in range(8)]
        for k in range(8):
            raw[k] = raw[k] - tree([mult[j] * sub(low[j], k) for j in range(8)])
        w = v * recip
        for j in range(7, 0, -1):
            w = w - jnp.where(row < j, c[j] * recip, 0.0) * sub(w, j)
        ws = [sub(w, k) for k in range(8)]
        for h in range(g + 1, 16):
            left = first if h == g + 1 else [lane(mat[h], 8 * g + k) for k in range(8)]
            mat[h] = jnp.where(inside, 0.0, mat[h]) - tree([left[k] * ws[k] for k in range(8)])
        c = raw
    return upper, inv


def blk(i):
    return slice(NB * i, NB * i + NB)


def factor_blocks(a_ref, u_ref, d_ref, e_ref=None):
    for k in range(4):
        upper, inv = diag_factor([a_ref[NB * k + 8 * g : NB * k + 8 * g + 8, blk(k)] for g in range(16)])
        for g in range(16):
            u_ref[NB * k + 8 * g : NB * k + 8 * g + 8, blk(k)] = upper[g]
            d_ref[8 * g : 8 * g + 8, :] = inv[g]
        dinv = d_ref[...]
        for j in range(k + 1, 4):
            u_ref[blk(k), blk(j)] = nn(dinv, a_ref[blk(k), blk(j)], HI)
        for i in range(k + 1, 4):
            a_ref[blk(i), NB * i :] -= tn(u_ref[blk(k), blk(i)], u_ref[blk(k), NB * i :], HI)
        if e_ref is not None:
            if k:
                e_ref[blk(k), : NB * k] = nn(dinv, e_ref[blk(k), : NB * k], HI)
            e_ref[blk(k), blk(k)] = dinv
            for i in range(k + 1, 4):
                e_ref[blk(i), : NB * (k + 1)] -= tn(u_ref[blk(k), blk(i)], e_ref[blk(k), : NB * (k + 1)], HI)


def gram_kernel(ids, c_ref, own_ref, oth_ref, g_ref):
    k = ids[1]
    pair = lax.rem(ids[2], 2)
    row = lax.broadcasted_iota(jnp.int32, (8, NB), 0)
    col = lax.broadcasted_iota(jnp.int32, (8, NB), 1)
    acc = jnp.zeros((8, NB), f32)
    for b in range(4):
        part = c_ref[:, WB * b : WB * b + WB]
        for i in range(4):
            g_ref[blk(i), NB * i :] = tn(part[:, blk(i)], part[:, NB * i :])
        for i in range(4):
            for g in range(16):
                tile = g_ref[NB * i + 8 * g : NB * i + 8 * g + 8, blk(i)]
                acc = acc + jnp.where(col == row + 8 * g, tile, 0.0)
        for ref, side in ((own_ref, k), (oth_ref, 1 - k)):
            for p, (i, j) in enumerate(PAIRS):
                for q in range(4):
                    start = pl.multiple_of(NB * i + 32 * q + 16 * pair + 8 * side, 8)
                    ref[b, 4 * p + q] = g_ref[pl.ds(start, 8), blk(j)]
    for b in range(4):
        own_ref[b, 4 * NP] = acc
        oth_ref[b, 4 * NP] = acc


def chol_kernel(scale, lam_scale, ids, p00, p01, p10, p11, s0, s1, s2, s3, o_ref, h_ref, a_ref, u_ref, d_ref):
    k = ids[1]
    pair = lax.rem(ids[2], 2)
    total = jnp.sum(s0[...] + s1[...] + s2[...] + s3[...], keepdims=True)
    lam = jnp.broadcast_to(total * lam_scale, (8, NB))
    row = lax.broadcasted_iota(jnp.int32, (8, NB), 0)
    col = lax.broadcasted_iota(jnp.int32, (8, NB), 1)
    for ref, flip_pair, flip_core in ((p00, 0, 0), (p01, 0, 1), (p10, 1, 0), (p11, 1, 1)):
        offset = 16 * lax.rem(pair + flip_pair, 2) + 8 * lax.rem(k + flip_core, 2)
        for p, (i, j) in enumerate(PAIRS):
            for q in range(4):
                tile = ref[4 * p + q] * scale
                if i == j:
                    tile = tile + jnp.where(col == row + (32 * q + offset), lam, 0.0)
                a_ref[pl.ds(pl.multiple_of(NB * i + 32 * q + offset, 8), 8), blk(j)] = tile
    factor_blocks(a_ref, u_ref, d_ref)
    for p, (i, j) in enumerate(PAIRS):
        o_ref[p] = u_ref[blk(i), blk(j)].astype(bf16)
    h_ref[...] = o_ref[pl.ds(HALF * k, HALF)]


def mixed_kernel(ids, own, r1, r2, r3, t1, t2, t3, sk_ref, w_ref, y_ref, p_ref, f_ref):
    x, k = ids[0], ids[1]
    zero = jnp.zeros((NB, NB), bf16)
    total = None
    for s, pieces in enumerate((((own, 0), (own, 1)), ((r1, 0), (t1, 1)), ((r2, 0), (t2, 1)), ((r3, 0), (t3, 1)))):
        for i in range(4):
            for j in range(i):
                f_ref[s, blk(i), blk(j)] = zero
        for ref, other in pieces:
            side = lax.rem(k + other, 2)
            for q in range(HALF):
                (i0, j0), (i1, j1) = PAIRS[q], PAIRS[HALF + q]
                i = pl.multiple_of(NB * (i0 + side * (i1 - i0)), NB)
                j = pl.multiple_of(NB * (j0 + side * (j1 - j0)), NB)
                block = ref[HALF * side + q] if s == 0 else ref[q]
                f_ref[s, pl.ds(i, NB), pl.ds(j, NB)] = block
                p_ref[s, HALF * side + q] = block
        cols = pl.ds(pl.multiple_of(WB * lax.rem(x - s + 4, 4), WB), WB)
        mixed = nn(sk_ref[:, cols], f_ref[s]).astype(bf16)
        y = nt(w_ref[:, cols], mixed)
        total = y if s == 0 else total + y
    n = y_ref.shape[1]
    for c in range(4):
        y_ref[c] = total[n * c : n * c + n, :].astype(y_ref.dtype)


def cross_kernel(ids, y_ref, own_ref, oth_ref, ys_ref):
    k = ids[1]
    y0, y1, y2, y3 = (y_ref[c].astype(f32) for c in range(4))
    y = ((y0 + y1) + (y2 + y3)).astype(bf16)
    ys_ref[...] = y
    for side in range(2):
        blocks = [tn(y[:, blk(i)], y[:, blk(j)]) for i, j in PAIRS[HALF * side : HALF * side + HALF]]

        def put(ref, blocks=blocks):
            for q, c in enumerate(blocks):
                for g in range(16):
                    ref[g, q] = c[8 * g : 8 * g + 8, :]

        pl.when(k == side)(lambda: put(own_ref))
        pl.when(k != side)(lambda: put(oth_ref))


def chol2_kernel(scale, ids, own_ref, oth_ref, o_ref, a_ref, u_ref, d_ref):
    k = ids[1]

    def put(first, second):
        for side, ref in enumerate((first, second)):
            for q, (i, j) in enumerate(PAIRS[HALF * side : HALF * side + HALF]):
                for g in range(16):
                    a_ref[NB * i + 8 * g : NB * i + 8 * g + 8, blk(j)] = ref[g, q] * scale

    pl.when(k == 0)(lambda: put(own_ref, oth_ref))
    pl.when(k != 0)(lambda: put(oth_ref, own_ref))
    o_ref[...] = jnp.zeros((WB, WB), f32)
    factor_blocks(a_ref, u_ref, d_ref, o_ref)


def moment_part(x, side, yb_ref, w_ref):
    cols = pl.ds(pl.multiple_of(256 * (2 * x + side), 256), 256)
    return tn(yb_ref[...], w_ref[:, cols])


def send_kernel(ids, y0, y1, y2, y3, w_ref, oth_ref, yb_ref, yf_ref):
    n = y0.shape[0]
    for s, ref in enumerate((y0, y1, y2, y3)):
        start = pl.multiple_of(lax.rem(ids[3] - s + 4, 4) * n, 8)
        yf_ref[pl.ds(start, n), :] = ref[...].astype(f32)
    yb_ref[...] = yf_ref[...].astype(bf16)
    for x in range(4):
        oth_ref[x] = moment_part(x, 1 - ids[1], yb_ref, w_ref).astype(bf16)


def keep_kernel(ids, yb_ref, w_ref, own_ref):
    for x in range(4):
        own_ref[x] = moment_part(x, ids[1], yb_ref, w_ref).astype(bf16)


def split(v):
    hi = v.astype(bf16)
    rest = v - hi.astype(f32)
    mid = rest.astype(bf16)
    return hi, mid, (rest - mid.astype(f32)).astype(bf16)


def part_kernel(inv_ref, s_ref, o_ref):
    s = s_ref[0]
    hi, mid, low = (nn(v, s) for v in split(inv_ref[...]))
    m = hi + (mid + low)
    for d in range(64):
        rows = m[8 * d : 8 * d + 8, :]
        o_ref[d] = jnp.concatenate([rows[:, :NB], rows[:, NB:]], axis=0).astype(bf16)


def panel_kernel(inv_ref, y_ref, o_ref):
    y = y_ref[...]
    hi, mid, low = (nt(y, v) for v in split(inv_ref[...]))
    o_ref[...] = hi + (mid + low)


def final_kernel(scale, ids, m_ref, p_ref, o_ref, mom_ref, f_ref):
    x = ids[0]
    zero = jnp.zeros((NB, NB), bf16)
    for m in range(8):
        t = [m_ref[8 * m + r].astype(f32) for r in range(8)]
        both = tree(t) * scale
        mom_ref[:, blk(2 * m)] = both[:8]
        mom_ref[:, blk(2 * m + 1)] = both[8:]
    for s in range(4):
        for i in range(4):
            for j in range(i):
                f_ref[s, blk(i), blk(j)] = zero
        for p, (i, j) in enumerate(PAIRS):
            f_ref[s, blk(i), blk(j)] = p_ref[s, p]
        cols = pl.ds(pl.multiple_of(WB * lax.rem(x - s + 4, 4), WB), WB)
        terms = jnp.concatenate([v.astype(f32) for v in split(mom_ref[:, cols])], axis=0).astype(bf16)
        p = nt(terms, f_ref[s])
        o_ref[:, cols] = p[:8] + (p[8:16] + p[16:])


def shift(v, axis, s, n):
    return lax.ppermute(v, axis, [(i, (i + s) % n) for i in range(n)])


def everyone(v, axis, n):
    return lax.all_to_all(jnp.broadcast_to(v[None], (n,) + v.shape), axis, 0, 0, tiled=True)


def shards(calib, weight, sketch):
    tokens = calib.shape[0] * 8
    width = calib.shape[1] * 4
    hidden = weight.shape[0] * 64
    ids = jnp.stack([lax.axis_index(a) for a in ("x", "core", "row", "col")]).astype(jnp.int32)

    n = weight.shape[0] // 4
    square = pltpu.VMEM((WB, WB), f32)
    brief = pl.CostEstimate(flops=1, bytes_accessed=1, transcendentals=0)
    diag = pltpu.VMEM((NB, NB), f32)

    pieces = shape((4, 4 * NP + 1, 8, NB))
    own, oth = call(
        gram_kernel, (pieces, pieces), "sv", "vv", [square], "gram"
    )(ids, calib)
    slab = jnp.sum(lax.all_to_all(own + shift(oth, "core", 1, 2), "x", 0, 0, tiled=True), axis=0)
    trace = slab[4 * NP]
    traces = [trace] + [shift(trace, "col", s, 4) for s in (1, 2, 3)]
    p00 = slab[: 4 * NP]
    p10 = lax.ppermute(p00, "row", [(i, i ^ 1) for i in range(8)])
    p01 = shift(p00, "core", 1, 2)
    p10, *traces = lax.optimization_barrier([p10] + traces)
    p11 = shift(p10, "core", 1, 2)
    sk_all = lax.all_gather(sketch.T, "row", axis=0, tiled=True)

    def chol1(*refs):
        chol_kernel(1.0 / tokens, damping_ratio / (tokens * width), *refs)

    fac, fac_half = call(
        chol1,
        (shape((NP, NB, NB), bf16), shape((HALF, NB, NB), bf16)),
        "svvvvvvvv",
        "vv",
        [square, square, diag],
        "chol_gram",
    )(ids, p00, p01, p10, p11, *traces)
    fac_half, sk_all = lax.optimization_barrier((fac_half, sk_all))
    got = [shift(fac_half, "x", s, 4) for s in (1, 2, 3)]
    got_oth = [shift(v, "core", 1, 2) for v in got]
    ypart, factors = call(
        mixed_kernel,
        (shape((4, n, WB), bf16), shape((4, NP, NB, NB), bf16)),
        "s" + "v" * 9,
        "vv",
        [pltpu.VMEM((4, WB, WB), bf16)],
        "mixed",
    )(ids, fac, *got, *got_oth, sk_all, weight)

    ypieces = lax.all_to_all(ypart, "col", 0, 0, tiled=True)
    tri = shape((16, HALF, 8, NB))
    cown, coth, ysum = call(cross_kernel, (tri, tri, shape((n, WB), bf16)), "sv", "vvv", [], "cross")(ids, ypieces)
    ys = [shift(ysum, "col", s, 4) for s in (1, 2, 3)]
    half = cown + shift(coth, "core", 1, 2)
    piece = jnp.sum(lax.all_to_all(half, ("x", "col"), 0, 0, tiled=True), axis=0)
    *ys, _ = lax.optimization_barrier(ys + [piece])

    parts = (4, WB, 256)
    toth, yb = call(
        send_kernel,
        (shape(parts, bf16), shape((4 * n, WB), bf16)),
        "svvvvv",
        "vv",
        [pltpu.VMEM((4 * n, WB), f32)],
        "moments_send",
        cost=brief,
    )(ids, ysum, *ys, weight)
    town = call(keep_kernel, shape(parts, bf16), "svv", "v", [], "moments_keep", cost=brief)(ids, yb, weight)
    t = (town.astype(f32) + shift(toth, "core", 1, 2).astype(f32)).astype(bf16)
    piece = jnp.sum(everyone(piece, "row", 8), axis=0)
    piece, t = lax.optimization_barrier((piece, t))
    t = lax.psum_scatter(t, "x", scatter_dimension=0, tiled=True)
    half = everyone(piece, ("x", "col"), 16)
    coth = shift(half, "core", 1, 2)

    def chol2(*refs):
        chol2_kernel(1.0 / hidden, *refs)

    inv = call(chol2, shape((WB, WB)), "svv", "v", [square, square, diag], "chol_cross")(ids, half, coth)
    parts = call(part_kernel, shape((64, 16, NB), bf16), "vv", "v", [], "project")(inv, t)
    parts = lax.all_to_all(parts, ("x", "core", "row"), 0, 0, tiled=True)

    def final(*refs):
        final_kernel(1.0 / math.sqrt(hidden), *refs)

    projections = call(final, shape((8, 4 * WB)), "svv", "v", [pltpu.VMEM((8, 4 * WB), f32), pltpu.VMEM((4, WB, WB), bf16)], "final")(
        ids, parts, factors
    )
    panels = call(panel_kernel, shape((4 * n, WB)), "vv", "v", [], "panels")(inv, yb)
    return (panels, projections)


def solution(mesh):
    fine = jax.sharding.Mesh(mesh.devices.reshape(4, 2, 8, 4), ("x", "core", "row", "col"))
    return jax.shard_map(
        shards,
        mesh=fine,
        in_specs=(P(("x", "core"), "col"), P(("x", "core", "row"), "col"), P("col", "row")),
        out_specs=(P(("x", "core", "row"), None), P(("x", "core", "row"), "col")),
        check_vma=False,
    )
```

```python
import math

import jax
import jax.numpy as jnp
from jax import lax
from jax.experimental import pallas as pl
from jax.experimental.pallas import tpu as pltpu
from jax.sharding import PartitionSpec as P

WB = 512
NB = 128
damping_ratio = 0.5
f32 = jnp.float32
bf16 = jnp.bfloat16
HI = lax.Precision.HIGHEST
PAIRS = [(i, j) for i in range(4) for j in range(i, 4)]
NP = len(PAIRS)
HALF = NP // 2


def tn(a, b, precision=None):
    return lax.dot_general(
        a, b, (((0,), (0,)), ((), ())), preferred_element_type=f32, precision=precision
    )


def nt(a, b, precision=None):
    return lax.dot_general(
        a, b, (((1,), (1,)), ((), ())), preferred_element_type=f32, precision=precision
    )


def nn(a, b, precision=None):
    return jnp.dot(a, b, preferred_element_type=f32, precision=precision)


SPACES = {"s": pltpu.SMEM, "v": pltpu.VMEM, "a": pl.ANY, "h": pltpu.HBM}


def call(kernel, out_shape, ins, outs, scratch=(), name=None, mib=16, cost=None):
    one = not isinstance(out_shape, (tuple, list))
    out_specs = tuple(pl.BlockSpec(memory_space=SPACES[c]) for c in outs)
    return pl.pallas_call(
        kernel,
        out_shape=out_shape,
        in_specs=[pl.BlockSpec(memory_space=SPACES[c]) for c in ins],
        out_specs=out_specs[0] if one else out_specs,
        scratch_shapes=list(scratch),
        compiler_params=pltpu.CompilerParams(vmem_limit_bytes=mib * 2**20),
        name=name,
        cost_estimate=cost,
    )


def shape(s, d=f32):
    return jax.ShapeDtypeStruct(s, d)


def sub(x, j):
    return jnp.broadcast_to(x[j : j + 1, :], (8, NB))


def lane(x, c):
    return jnp.broadcast_to(x[:, c : c + 1], (8, NB))


def tree(t):
    return ((t[0] + t[1]) + (t[2] + t[3])) + ((t[4] + t[5]) + (t[6] + t[7]))


def diag_factor(rows):
    row = lax.broadcasted_iota(jnp.int32, (8, NB), 0)
    col = lax.broadcasted_iota(jnp.int32, (8, NB), 1)
    mat = list(rows)
    upper, inv = [], []
    c = [lane(mat[0], j) for j in range(8)]
    for g in range(16):
        inside = (col >= 8 * g) & (col < 8 * g + 8)
        v = jnp.where(inside, jnp.where(col == row + 8 * g, 1.0, 0.0), mat[g])
        rs, q = [], {}
        root = jnp.zeros((8, NB), f32)
        recip = root
        for j in range(8):
            p = sub(c[j], j)
            r = 1.0 / p
            below = jnp.where(row > j, c[j], 0.0)
            for k in range(j + 1, 8):
                q[j, k] = sub(c[k], j)
                c[k] = c[k] - (below * q[j, k]) * r
            v = v - below * (sub(v, j) * r)
            root = jnp.where(row == j, lax.rsqrt(p), root)
            recip = jnp.where(row == j, r, recip)
            rs.append(r)
        scaled = v * root
        own = jnp.zeros((8, NB), f32)
        for k in range(8):
            own = jnp.where(col == 8 * g + k, c[k], own)
        own = jnp.where(col >= row + 8 * g, own * root, 0.0)
        upper.append(jnp.where(col >= 8 * g + 8, scaled, own))
        inv.append(jnp.where(col < 8 * g + 8, scaled, 0.0))
        if g == 15:
            break
        raw = [lane(mat[g + 1], 8 * g + 8 + k) for k in range(8)]
        first = [lane(mat[g + 1], 8 * g + k) for k in range(8)]
        low = []
        for j in range(8):
            t = first[j]
            for i in range(j):
                t = t - low[i] * (q[i, j] * rs[i])
            low.append(t)
        mult = [low[j] * rs[j] for j in range(8)]
        for k in range(8):
            raw[k] = raw[k] - tree([mult[j] * sub(low[j], k) for j in range(8)])
        w = v * recip
        for j in range(7, 0, -1):
            w = w - jnp.where(row < j, c[j] * recip, 0.0) * sub(w, j)
        ws = [sub(w, k) for k in range(8)]
        for h in range(g + 1, 16):
            left = first if h == g + 1 else [lane(mat[h], 8 * g + k) for k in range(8)]
            mat[h] = jnp.where(inside, 0.0, mat[h]) - tree([left[k] * ws[k] for k in range(8)])
        c = raw
    return upper, inv


def blk(i):
    return slice(NB * i, NB * i + NB)


def factor_blocks(a_ref, u_ref, d_ref, e_ref=None):
    for k in range(4):
        upper, inv = diag_factor([a_ref[NB * k + 8 * g : NB * k + 8 * g + 8, blk(k)] for g in range(16)])
        for g in range(16):
            u_ref[NB * k + 8 * g : NB * k + 8 * g + 8, blk(k)] = upper[g]
            d_ref[8 * g : 8 * g + 8, :] = inv[g]
        dinv = d_ref[...]
        for j in range(k + 1, 4):
            u_ref[blk(k), blk(j)] = nn(dinv, a_ref[blk(k), blk(j)], HI)
        for i in range(k + 1, 4):
            a_ref[blk(i), NB * i :] -= tn(u_ref[blk(k), blk(i)], u_ref[blk(k), NB * i :], HI)
        if e_ref is not None:
            if k:
                e_ref[blk(k), : NB * k] = nn(dinv, e_ref[blk(k), : NB * k], HI)
            e_ref[blk(k), blk(k)] = dinv
            for i in range(k + 1, 4):
                e_ref[blk(i), : NB * (k + 1)] -= tn(u_ref[blk(k), blk(i)], e_ref[blk(k), : NB * (k + 1)], HI)


def gram_kernel(ids, c_ref, own_ref, oth_ref, g_ref):
    k = ids[1]
    pair = lax.rem(ids[2], 2)
    row = lax.broadcasted_iota(jnp.int32, (8, NB), 0)
    col = lax.broadcasted_iota(jnp.int32, (8, NB), 1)
    acc = jnp.zeros((8, NB), f32)
    for b in range(4):
        part = c_ref[:, WB * b : WB * b + WB]
        for i in range(4):
            g_ref[blk(i), NB * i :] = tn(part[:, blk(i)], part[:, NB * i :])
        for i in range(4):
            for g in range(16):
                tile = g_ref[NB * i + 8 * g : NB * i + 8 * g + 8, blk(i)]
                acc = acc + jnp.where(col == row + 8 * g, tile, 0.0)
        for ref, side in ((own_ref, k), (oth_ref, 1 - k)):
            for p, (i, j) in enumerate(PAIRS):
                for q in range(4):
                    start = pl.multiple_of(NB * i + 32 * q + 16 * pair + 8 * side, 8)
                    ref[b, 4 * p + q] = g_ref[pl.ds(start, 8), blk(j)]
    for b in range(4):
        own_ref[b, 4 * NP] = acc
        oth_ref[b, 4 * NP] = acc


def chol_kernel(scale, lam_scale, ids, p00, p01, p10, p11, s0, s1, s2, s3, o_ref, h_ref, a_ref, u_ref, d_ref):
    k = ids[1]
    pair = lax.rem(ids[2], 2)
    total = jnp.sum(s0[...] + s1[...] + s2[...] + s3[...], keepdims=True)
    lam = jnp.broadcast_to(total * lam_scale, (8, NB))
    row = lax.broadcasted_iota(jnp.int32, (8, NB), 0)
    col = lax.broadcasted_iota(jnp.int32, (8, NB), 1)
    for ref, flip_pair, flip_core in ((p00, 0, 0), (p01, 0, 1), (p10, 1, 0), (p11, 1, 1)):
        offset = 16 * lax.rem(pair + flip_pair, 2) + 8 * lax.rem(k + flip_core, 2)
        for p, (i, j) in enumerate(PAIRS):
            for q in range(4):
                tile = ref[4 * p + q] * scale
                if i == j:
                    tile = tile + jnp.where(col == row + (32 * q + offset), lam, 0.0)
                a_ref[pl.ds(pl.multiple_of(NB * i + 32 * q + offset, 8), 8), blk(j)] = tile
    factor_blocks(a_ref, u_ref, d_ref)
    for p, (i, j) in enumerate(PAIRS):
        o_ref[p] = u_ref[blk(i), blk(j)].astype(bf16)
    h_ref[...] = o_ref[pl.ds(HALF * k, HALF)]


def mixed_part(ids, s, pieces, sk_ref, w_ref, p_ref, f_ref):
    x, k = ids[0], ids[1]
    whole = len(pieces) == 1
    n = s % 2
    for i in range(4):
        for j in range(i):
            f_ref[n, blk(i), blk(j)] = jnp.zeros((NB, NB), bf16)
    for other in range(2):
        side = lax.rem(k + other, 2)
        for q in range(HALF):
            (i0, j0), (i1, j1) = PAIRS[q], PAIRS[HALF + q]
            i = pl.multiple_of(NB * (i0 + side * (i1 - i0)), NB)
            j = pl.multiple_of(NB * (j0 + side * (j1 - j0)), NB)
            block = pieces[0][HALF * side + q] if whole else pieces[other][q]
            f_ref[n, pl.ds(i, NB), pl.ds(j, NB)] = block
            p_ref[n, HALF * side + q] = block
    cols = pl.ds(pl.multiple_of(WB * lax.rem(x - s + 4, 4), WB), WB)
    mixed = nn(sk_ref[:, cols], f_ref[n]).astype(bf16)
    return nt(w_ref[:, cols], mixed)


def mixed_first_kernel(ids, own, r3, t3, sk_ref, w_ref, y_ref, p_ref, f_ref):
    y = mixed_part(ids, 0, (own,), sk_ref, w_ref, p_ref, f_ref)
    y_ref[...] = y + mixed_part(ids, 3, (r3, t3), sk_ref, w_ref, p_ref, f_ref)


def mixed_kernel(ids, r1, t1, r2, t2, sk_ref, w_ref, before_ref, y_ref, p_ref, f_ref):
    y = before_ref[...] + mixed_part(ids, 2, (r2, t2), sk_ref, w_ref, p_ref, f_ref)
    y = y + mixed_part(ids, 1, (r1, t1), sk_ref, w_ref, p_ref, f_ref)
    n = y_ref.shape[1]
    for c in range(4):
        y_ref[c] = y[n * c : n * c + n, :].astype(y_ref.dtype)


def stage_kernel(s_ref, o_ref, sem):
    copy = pltpu.make_async_copy(s_ref, o_ref, sem)
    copy.start()
    copy.wait()


def cross_kernel(ids, y_ref, own_ref, oth_ref, ys_ref):
    k = ids[1]
    y0, y1, y2, y3 = (y_ref[c].astype(f32) for c in range(4))
    y = ((y0 + y1) + (y2 + y3)).astype(bf16)
    ys_ref[...] = y
    for side in range(2):
        blocks = [tn(y[:, blk(i)], y[:, blk(j)]) for i, j in PAIRS[HALF * side : HALF * side + HALF]]

        def put(ref, blocks=blocks):
            for q, c in enumerate(blocks):
                for g in range(16):
                    ref[g, q] = c[8 * g : 8 * g + 8, :]

        pl.when(k == side)(lambda: put(own_ref))
        pl.when(k != side)(lambda: put(oth_ref))


def chol2_kernel(scale, ids, own_ref, oth_ref, o_ref, a_ref, u_ref, d_ref):
    k = ids[1]

    def put(first, second):
        for side, ref in enumerate((first, second)):
            for q, (i, j) in enumerate(PAIRS[HALF * side : HALF * side + HALF]):
                for g in range(16):
                    a_ref[NB * i + 8 * g : NB * i + 8 * g + 8, blk(j)] = ref[g, q] * scale

    pl.when(k == 0)(lambda: put(own_ref, oth_ref))
    pl.when(k != 0)(lambda: put(oth_ref, own_ref))
    o_ref[...] = jnp.zeros((WB, WB), f32)
    factor_blocks(a_ref, u_ref, d_ref, o_ref)


def moment_part(x, side, yb_ref, w_ref):
    cols = pl.ds(pl.multiple_of(256 * (2 * x + side), 256), 256)
    return tn(yb_ref[...], w_ref[:, cols])


def send_kernel(ids, y0, y1, y2, y3, w_ref, oth_ref, yb_ref, yf_ref):
    n = y0.shape[0]
    for s, ref in enumerate((y0, y1, y2, y3)):
        start = pl.multiple_of(lax.rem(ids[3] - s + 4, 4) * n, 8)
        yf_ref[pl.ds(start, n), :] = ref[...].astype(f32)
    yb_ref[...] = yf_ref[...].astype(bf16)
    for x in range(4):
        oth_ref[x] = moment_part(x, 1 - ids[1], yb_ref, w_ref).astype(bf16)


def keep_kernel(ids, yb_ref, w_ref, got_ref, o_ref):
    for x in range(4):
        t = moment_part(x, ids[1], yb_ref, w_ref)
        o_ref[x] = (t + got_ref[x].astype(f32)).astype(bf16)


def split(v):
    hi = v.astype(bf16)
    rest = v - hi.astype(f32)
    mid = rest.astype(bf16)
    return hi, mid, (rest - mid.astype(f32)).astype(bf16)


def part_kernel(inv_ref, s_ref, o_ref):
    s = s_ref[0]
    hi, mid, low = (nn(v, s) for v in split(inv_ref[...]))
    m = hi + (mid + low)
    for d in range(64):
        rows = m[8 * d : 8 * d + 8, :]
        o_ref[d] = jnp.concatenate([rows[:, :NB], rows[:, NB:]], axis=0).astype(bf16)


def panel_kernel(inv_ref, y_ref, o_ref):
    y = y_ref[...]
    hi, mid, low = (nt(y, v) for v in split(inv_ref[...]))
    o_ref[...] = hi + (mid + low)


def final_kernel(scale, ids, m_ref, first_ref, second_ref, o_ref, mom_ref):
    x = ids[0]
    for m in range(8):
        t = [m_ref[8 * m + r].astype(f32) for r in range(8)]
        both = tree(t) * scale
        mom_ref[:, blk(2 * m)] = both[:8]
        mom_ref[:, blk(2 * m + 1)] = both[8:]
    for s in range(4):
        cols = pl.ds(pl.multiple_of(WB * lax.rem(x - s + 4, 4), WB), WB)
        terms = jnp.concatenate([v.astype(f32) for v in split(mom_ref[:, cols])], axis=0).astype(bf16)
        outs = [None] * 4
        for p, (i, j) in enumerate(PAIRS):
            t = nt(terms[:, blk(j)], (first_ref if s in (0, 3) else second_ref)[s % 2, p])
            outs[i] = t if outs[i] is None else outs[i] + t
        o_ref[:, cols] = jnp.concatenate([t[:8] + (t[8:16] + t[16:]) for t in outs], axis=1)


def shift(v, axis, s, n):
    return lax.ppermute(v, axis, [(i, (i + s) % n) for i in range(n)])


def everyone(v, axis, n):
    return lax.all_to_all(jnp.broadcast_to(v[None], (n,) + v.shape), axis, 0, 0, tiled=True)


def shards(calib, weight, sketch):
    tokens = calib.shape[0] * 8
    width = calib.shape[1] * 4
    hidden = weight.shape[0] * 64
    ids = jnp.stack([lax.axis_index(a) for a in ("x", "core", "row", "col")]).astype(jnp.int32)

    n = weight.shape[0] // 4
    square = pltpu.VMEM((WB, WB), f32)
    brief = pl.CostEstimate(flops=1, bytes_accessed=1, transcendentals=0)
    diag = pltpu.VMEM((NB, NB), f32)

    pieces = shape((4, 4 * NP + 1, 8, NB))
    own, oth = call(
        gram_kernel, (pieces, pieces), "sv", "vv", [square], "gram"
    )(ids, calib)
    turned, oth = lax.optimization_barrier((sketch.T, oth))
    sk_all = lax.all_gather(turned, "row", axis=0, tiled=True)
    slab = jnp.sum(lax.all_to_all(own + shift(oth, "core", 1, 2), "x", 0, 0, tiled=True), axis=0)
    trace = slab[4 * NP]
    traces = [trace] + [shift(trace, "col", s, 4) for s in (1, 2, 3)]
    p00 = slab[: 4 * NP]
    p10 = lax.ppermute(p00, "row", [(i, i ^ 1) for i in range(8)])
    p01 = shift(p00, "core", 1, 2)
    p10, *traces = lax.optimization_barrier([p10] + traces)
    p11 = shift(p10, "core", 1, 2)

    def chol1(*refs):
        chol_kernel(1.0 / tokens, damping_ratio / (tokens * width), *refs)

    fac, fac_half = call(
        chol1,
        (shape((NP, NB, NB), bf16), shape((HALF, NB, NB), bf16)),
        "svvvvvvvv",
        "vv",
        [square, square, diag],
        "chol_gram",
    )(ids, p00, p01, p10, p11, *traces)
    sk_all = call(stage_kernel, shape(sk_all.shape, bf16), "a", "v", [pltpu.SemaphoreType.DMA], "stage")(sk_all)
    got = [shift(fac_half, "x", s, 4) for s in (1, 2, 3)]
    got_oth = [shift(v, "core", 1, 2) for v in got]
    pair_shape = shape((2, NP, NB, NB), bf16)
    unpacked = [pltpu.VMEM((2, WB, WB), bf16)]
    ypart, first = call(
        mixed_first_kernel, (shape((4 * n, WB)), pair_shape), "svvvvv", "vv", unpacked, "mixed_first"
    )(ids, fac, got[2], got_oth[2], sk_all, weight)
    ypart, second = call(
        mixed_kernel, (shape((4, n, WB), bf16), pair_shape), "s" + "v" * 7, "vv", unpacked, "mixed"
    )(ids, got[0], got_oth[0], got[1], got_oth[1], sk_all, weight, ypart)

    ypieces = lax.all_to_all(ypart, "col", 0, 0, tiled=True)
    tri = shape((16, HALF, 8, NB))
    cown, coth, ysum = call(cross_kernel, (tri, tri, shape((n, WB), bf16)), "sv", "vvv", [], "cross")(ids, ypieces)
    ys = [shift(ysum, "col", s, 4) for s in (1, 2, 3)]
    half = cown + shift(coth, "core", 1, 2)
    piece = jnp.sum(lax.all_to_all(half, ("x", "col"), 0, 0, tiled=True), axis=0)
    *ys, _ = lax.optimization_barrier(ys + [piece])

    parts = (4, WB, 256)
    toth, yb = call(
        send_kernel,
        (shape(parts, bf16), shape((4 * n, WB), bf16)),
        "svvvvv",
        "vv",
        [pltpu.VMEM((4 * n, WB), f32)],
        "moments_send",
        cost=brief,
    )(ids, ysum, *ys, weight)
    t = call(keep_kernel, shape(parts, bf16), "svvv", "v", [], "moments_keep", cost=brief)(
        ids, yb, weight, shift(toth, "core", 1, 2)
    )
    piece = jnp.sum(everyone(piece, "row", 8), axis=0)
    piece, t = lax.optimization_barrier((piece, t))
    t = lax.psum_scatter(t, "x", scatter_dimension=0, tiled=True)
    half = everyone(piece, ("x", "col"), 16)
    coth = shift(half, "core", 1, 2)

    def chol2(*refs):
        chol2_kernel(1.0 / hidden, *refs)

    inv = call(chol2, shape((WB, WB)), "svv", "v", [square, square, diag], "chol_cross")(ids, half, coth)
    parts = call(part_kernel, shape((64, 16, NB), bf16), "vv", "v", [], "project")(inv, t)
    parts = lax.all_to_all(parts, ("x", "core", "row"), 0, 0, tiled=True)

    def final(*refs):
        final_kernel(1.0 / math.sqrt(hidden), *refs)

    projections = call(final, shape((8, 4 * WB)), "svvv", "v", [pltpu.VMEM((8, 4 * WB), f32)], "final")(
        ids, parts, first, second
    )
    panels = call(panel_kernel, shape((4 * n, WB)), "vv", "v", [], "panels")(inv, yb)
    return (panels, projections)


def solution(mesh):
    fine = jax.sharding.Mesh(mesh.devices.reshape(4, 2, 8, 4), ("x", "core", "row", "col"))
    return jax.shard_map(
        shards,
        mesh=fine,
        in_specs=(P(("x", "core"), "col"), P(("x", "core", "row"), "col"), P("col", "row")),
        out_specs=(P(("x", "core", "row"), None), P(("x", "core", "row"), "col")),
        check_vma=False,
    )
```

```python
import math

import jax
import jax.numpy as jnp
from jax import lax
from jax.experimental import pallas as pl
from jax.experimental.pallas import tpu as pltpu
from jax.sharding import PartitionSpec as P

WB = 512
NB = 128
damping_ratio = 0.5
f32 = jnp.float32
bf16 = jnp.bfloat16
HI = lax.Precision.HIGHEST
PAIRS = [(i, j) for i in range(4) for j in range(i, 4)]
NP = len(PAIRS)
HALF = NP // 2


def tn(a, b, precision=None):
    return lax.dot_general(
        a, b, (((0,), (0,)), ((), ())), preferred_element_type=f32, precision=precision
    )


def nt(a, b, precision=None):
    return lax.dot_general(
        a, b, (((1,), (1,)), ((), ())), preferred_element_type=f32, precision=precision
    )


def nn(a, b, precision=None):
    return jnp.dot(a, b, preferred_element_type=f32, precision=precision)


SPACES = {"s": pltpu.SMEM, "v": pltpu.VMEM, "a": pl.ANY, "h": pltpu.HBM}


def call(kernel, out_shape, ins, outs, scratch=(), name=None, mib=16, cost=None):
    one = not isinstance(out_shape, (tuple, list))
    out_specs = tuple(pl.BlockSpec(memory_space=SPACES[c]) for c in outs)
    return pl.pallas_call(
        kernel,
        out_shape=out_shape,
        in_specs=[pl.BlockSpec(memory_space=SPACES[c]) for c in ins],
        out_specs=out_specs[0] if one else out_specs,
        scratch_shapes=list(scratch),
        compiler_params=pltpu.CompilerParams(vmem_limit_bytes=mib * 2**20),
        name=name,
        cost_estimate=cost,
    )


def shape(s, d=f32):
    return jax.ShapeDtypeStruct(s, d)


def sub(x, j):
    return jnp.broadcast_to(x[j : j + 1, :], (8, NB))


def lane(x, c):
    return jnp.broadcast_to(x[:, c : c + 1], (8, NB))


def tree(t):
    return ((t[0] + t[1]) + (t[2] + t[3])) + ((t[4] + t[5]) + (t[6] + t[7]))


def diag_factor(rows):
    row = lax.broadcasted_iota(jnp.int32, (8, NB), 0)
    col = lax.broadcasted_iota(jnp.int32, (8, NB), 1)
    mat = list(rows)
    upper, inv = [], []
    c = [lane(mat[0], j) for j in range(8)]
    for g in range(16):
        inside = (col >= 8 * g) & (col < 8 * g + 8)
        v = jnp.where(inside, jnp.where(col == row + 8 * g, 1.0, 0.0), mat[g])
        rs, q = [], {}
        root = jnp.zeros((8, NB), f32)
        recip = root
        for j in range(8):
            p = sub(c[j], j)
            r = 1.0 / p
            below = jnp.where(row > j, c[j], 0.0)
            for k in range(j + 1, 8):
                q[j, k] = sub(c[k], j)
                c[k] = c[k] - (below * q[j, k]) * r
            v = v - below * (sub(v, j) * r)
            root = jnp.where(row == j, lax.rsqrt(p), root)
            recip = jnp.where(row == j, r, recip)
            rs.append(r)
        scaled = v * root
        own = jnp.zeros((8, NB), f32)
        for k in range(8):
            own = jnp.where(col == 8 * g + k, c[k], own)
        own = jnp.where(col >= row + 8 * g, own * root, 0.0)
        upper.append(jnp.where(col >= 8 * g + 8, scaled, own))
        inv.append(jnp.where(col < 8 * g + 8, scaled, 0.0))
        if g == 15:
            break
        raw = [lane(mat[g + 1], 8 * g + 8 + k) for k in range(8)]
        first = [lane(mat[g + 1], 8 * g + k) for k in range(8)]
        low = []
        for j in range(8):
            t = first[j]
            for i in range(j):
                t = t - low[i] * (q[i, j] * rs[i])
            low.append(t)
        mult = [low[j] * rs[j] for j in range(8)]
        for k in range(8):
            raw[k] = raw[k] - tree([mult[j] * sub(low[j], k) for j in range(8)])
        w = v * recip
        for j in range(7, 0, -1):
            w = w - jnp.where(row < j, c[j] * recip, 0.0) * sub(w, j)
        ws = [sub(w, k) for k in range(8)]
        for h in range(g + 1, 16):
            left = first if h == g + 1 else [lane(mat[h], 8 * g + k) for k in range(8)]
            mat[h] = jnp.where(inside, 0.0, mat[h]) - tree([left[k] * ws[k] for k in range(8)])
        c = raw
    return upper, inv


def blk(i):
    return slice(NB * i, NB * i + NB)


def factor_blocks(a_ref, u_ref, d_ref, e_ref=None):
    for k in range(4):
        upper, inv = diag_factor([a_ref[NB * k + 8 * g : NB * k + 8 * g + 8, blk(k)] for g in range(16)])
        for g in range(16):
            u_ref[NB * k + 8 * g : NB * k + 8 * g + 8, blk(k)] = upper[g]
            d_ref[8 * g : 8 * g + 8, :] = inv[g]
        dinv = d_ref[...]
        for j in range(k + 1, 4):
            u_ref[blk(k), blk(j)] = nn(dinv, a_ref[blk(k), blk(j)], HI)
        for i in range(k + 1, 4):
            a_ref[blk(i), NB * i :] -= tn(u_ref[blk(k), blk(i)], u_ref[blk(k), NB * i :], HI)
        if e_ref is not None:
            if k:
                e_ref[blk(k), : NB * k] = nn(dinv, e_ref[blk(k), : NB * k], HI)
            e_ref[blk(k), blk(k)] = dinv
            for i in range(k + 1, 4):
                e_ref[blk(i), : NB * (k + 1)] -= tn(u_ref[blk(k), blk(i)], e_ref[blk(k), : NB * (k + 1)], HI)


def gram_kernel(ids, c_ref, own_ref, oth_ref, g_ref):
    k = ids[1]
    pair = lax.rem(ids[2], 2)
    row = lax.broadcasted_iota(jnp.int32, (8, NB), 0)
    col = lax.broadcasted_iota(jnp.int32, (8, NB), 1)
    acc = jnp.zeros((8, NB), f32)
    for b in range(4):
        part = c_ref[:, WB * b : WB * b + WB]
        for i in range(4):
            g_ref[blk(i), NB * i :] = tn(part[:, blk(i)], part[:, NB * i :])
        for i in range(4):
            for g in range(16):
                tile = g_ref[NB * i + 8 * g : NB * i + 8 * g + 8, blk(i)]
                acc = acc + jnp.where(col == row + 8 * g, tile, 0.0)
        for ref, side in ((own_ref, k), (oth_ref, 1 - k)):
            for p, (i, j) in enumerate(PAIRS):
                for q in range(4):
                    start = pl.multiple_of(NB * i + 32 * q + 16 * pair + 8 * side, 8)
                    ref[b, 4 * p + q] = g_ref[pl.ds(start, 8), blk(j)]
    for b in range(4):
        own_ref[b, 4 * NP] = acc
        oth_ref[b, 4 * NP] = acc


def chol_kernel(scale, lam_scale, ids, p00, p01, p10, p11, s0, s1, s2, s3, o_ref, h_ref, a_ref, u_ref, d_ref):
    k = ids[1]
    pair = lax.rem(ids[2], 2)
    total = jnp.sum(s0[...] + s1[...] + s2[...] + s3[...], keepdims=True)
    lam = jnp.broadcast_to(total * lam_scale, (8, NB))
    row = lax.broadcasted_iota(jnp.int32, (8, NB), 0)
    col = lax.broadcasted_iota(jnp.int32, (8, NB), 1)
    for ref, flip_pair, flip_core in ((p00, 0, 0), (p01, 0, 1), (p10, 1, 0), (p11, 1, 1)):
        offset = 16 * lax.rem(pair + flip_pair, 2) + 8 * lax.rem(k + flip_core, 2)
        for p, (i, j) in enumerate(PAIRS):
            for q in range(4):
                tile = ref[4 * p + q] * scale
                if i == j:
                    tile = tile + jnp.where(col == row + (32 * q + offset), lam, 0.0)
                a_ref[pl.ds(pl.multiple_of(NB * i + 32 * q + offset, 8), 8), blk(j)] = tile
    factor_blocks(a_ref, u_ref, d_ref)
    for p, (i, j) in enumerate(PAIRS):
        o_ref[p] = u_ref[blk(i), blk(j)].astype(bf16)
    h_ref[...] = o_ref[pl.ds(HALF * k, HALF)]


def mixed_part(ids, s, pieces, sk_ref, w_ref, p_ref, f_ref):
    x, k = ids[0], ids[1]
    whole = len(pieces) == 1
    n = s % 2
    for i in range(4):
        for j in range(i):
            f_ref[n, blk(i), blk(j)] = jnp.zeros((NB, NB), bf16)
    for other in range(2):
        side = lax.rem(k + other, 2)
        for q in range(HALF):
            (i0, j0), (i1, j1) = PAIRS[q], PAIRS[HALF + q]
            i = pl.multiple_of(NB * (i0 + side * (i1 - i0)), NB)
            j = pl.multiple_of(NB * (j0 + side * (j1 - j0)), NB)
            block = pieces[0][HALF * side + q] if whole else pieces[other][q]
            f_ref[n, pl.ds(i, NB), pl.ds(j, NB)] = block
            p_ref[n, HALF * side + q] = block
    cols = pl.ds(pl.multiple_of(WB * lax.rem(x - s + 4, 4), WB), WB)
    mixed = nn(sk_ref[:, cols], f_ref[n]).astype(bf16)
    return nt(w_ref[:, cols], mixed)


def mixed_first_kernel(ids, own, r3, t3, sk_ref, w_ref, y_ref, p_ref, f_ref):
    y = mixed_part(ids, 0, (own,), sk_ref, w_ref, p_ref, f_ref)
    y_ref[...] = y + mixed_part(ids, 3, (r3, t3), sk_ref, w_ref, p_ref, f_ref)


def mixed_kernel(ids, r1, t1, r2, t2, sk_ref, w_ref, before_ref, y_ref, p_ref, f_ref):
    y = before_ref[...] + mixed_part(ids, 2, (r2, t2), sk_ref, w_ref, p_ref, f_ref)
    y = y + mixed_part(ids, 1, (r1, t1), sk_ref, w_ref, p_ref, f_ref)
    n = y_ref.shape[1]
    for c in range(4):
        y_ref[c] = y[n * c : n * c + n, :].astype(y_ref.dtype)


def stage_kernel(s_ref, o_ref, sem):
    copy = pltpu.make_async_copy(s_ref, o_ref, sem)
    copy.start()
    copy.wait()


def cross_kernel(ids, y_ref, own_ref, oth_ref, ys_ref):
    k = ids[1]
    y0, y1, y2, y3 = (y_ref[c].astype(f32) for c in range(4))
    y = ((y0 + y1) + (y2 + y3)).astype(bf16)
    ys_ref[...] = y
    for side in range(2):
        blocks = [tn(y[:, blk(i)], y[:, blk(j)]) for i, j in PAIRS[HALF * side : HALF * side + HALF]]

        def put(ref, blocks=blocks):
            for q, c in enumerate(blocks):
                for g in range(16):
                    ref[g, q] = c[8 * g : 8 * g + 8, :]

        pl.when(k == side)(lambda: put(own_ref))
        pl.when(k != side)(lambda: put(oth_ref))


def chol2_kernel(scale, ids, own_ref, oth_ref, o_ref, a_ref, u_ref, d_ref):
    k = ids[1]

    def put(first, second):
        for side, ref in enumerate((first, second)):
            for q, (i, j) in enumerate(PAIRS[HALF * side : HALF * side + HALF]):
                for g in range(16):
                    a_ref[NB * i + 8 * g : NB * i + 8 * g + 8, blk(j)] = ref[g, q] * scale

    pl.when(k == 0)(lambda: put(own_ref, oth_ref))
    pl.when(k != 0)(lambda: put(oth_ref, own_ref))
    o_ref[...] = jnp.zeros((WB, WB), f32)
    factor_blocks(a_ref, u_ref, d_ref, o_ref)


def moment_part(x, side, yb_ref, w_ref):
    cols = pl.ds(pl.multiple_of(256 * (2 * x + side), 256), 256)
    return tn(yb_ref[...], w_ref[:, cols])


def send_kernel(ids, y0, y1, y2, y3, w_ref, oth_ref, yb_ref, yf_ref):
    n = y0.shape[0]
    for s, ref in enumerate((y0, y1, y2, y3)):
        start = pl.multiple_of(lax.rem(ids[3] - s + 4, 4) * n, 8)
        yf_ref[pl.ds(start, n), :] = ref[...].astype(f32)
    yb_ref[...] = yf_ref[...].astype(bf16)
    for x in range(4):
        oth_ref[x] = moment_part(x, 1 - ids[1], yb_ref, w_ref).astype(bf16)


def keep_kernel(ids, yb_ref, w_ref, got_ref, o_ref):
    for x in range(4):
        t = moment_part(x, ids[1], yb_ref, w_ref)
        o_ref[x] = (t + got_ref[x].astype(f32)).astype(bf16)


def split(v):
    hi = v.astype(bf16)
    rest = v - hi.astype(f32)
    mid = rest.astype(bf16)
    return hi, mid, (rest - mid.astype(f32)).astype(bf16)


def part_kernel(inv_ref, s_ref, o_ref):
    s = s_ref[0]
    hi, mid, _ = split(inv_ref[...])
    m = nn(hi, s) + nn(mid, s)
    for d in range(64):
        rows = m[8 * d : 8 * d + 8, :]
        o_ref[d] = jnp.concatenate([rows[:, :NB], rows[:, NB:]], axis=0).astype(bf16)


def panel_kernel(inv_ref, y_ref, o_ref):
    y = y_ref[...]
    hi, mid, low = (nt(y, v) for v in split(inv_ref[...]))
    o_ref[...] = hi + (mid + low)


def final_kernel(scale, ids, m_ref, first_ref, second_ref, o_ref, mom_ref):
    x = ids[0]
    for m in range(8):
        t = [m_ref[8 * m + r].astype(f32) for r in range(8)]
        both = tree(t) * scale
        mom_ref[:, blk(2 * m)] = both[:8]
        mom_ref[:, blk(2 * m + 1)] = both[8:]
    for s in range(4):
        cols = pl.ds(pl.multiple_of(WB * lax.rem(x - s + 4, 4), WB), WB)
        terms = jnp.concatenate([v.astype(f32) for v in split(mom_ref[:, cols])], axis=0).astype(bf16)
        outs = [None] * 4
        for p, (i, j) in enumerate(PAIRS):
            t = nt(terms[:, blk(j)], (first_ref if s in (0, 3) else second_ref)[s % 2, p])
            outs[i] = t if outs[i] is None else outs[i] + t
        o_ref[:, cols] = jnp.concatenate([t[:8] + (t[8:16] + t[16:]) for t in outs], axis=1)


def shift(v, axis, s, n):
    return lax.ppermute(v, axis, [(i, (i + s) % n) for i in range(n)])


def everyone(v, axis, n):
    return lax.all_to_all(jnp.broadcast_to(v[None], (n,) + v.shape), axis, 0, 0, tiled=True)


def shards(calib, weight, sketch):
    tokens = calib.shape[0] * 8
    width = calib.shape[1] * 4
    hidden = weight.shape[0] * 64
    ids = jnp.stack([lax.axis_index(a) for a in ("x", "core", "row", "col")]).astype(jnp.int32)

    n = weight.shape[0] // 4
    square = pltpu.VMEM((WB, WB), f32)
    brief = pl.CostEstimate(flops=1, bytes_accessed=1, transcendentals=0)
    diag = pltpu.VMEM((NB, NB), f32)

    pieces = shape((4, 4 * NP + 1, 8, NB))
    own, oth = call(
        gram_kernel, (pieces, pieces), "sv", "vv", [square], "gram"
    )(ids, calib)
    turned, oth = lax.optimization_barrier((sketch.T, oth))
    sk_all = lax.all_gather(turned, "row", axis=0, tiled=True)
    slab = jnp.sum(lax.all_to_all(own + shift(oth, "core", 1, 2), "x", 0, 0, tiled=True), axis=0)
    trace = slab[4 * NP]
    ring = [(4 * k + y, 4 * k + (y + 1 + 2 * k) % 4) for k in range(2) for y in range(4)]
    side = lax.ppermute(trace, ("core", "col"), ring)
    far = shift(trace, "col", 2, 4)
    p00 = slab[: 4 * NP]
    p10 = lax.ppermute(p00, "row", [(i, i ^ 1) for i in range(8)])
    p01 = shift(p00, "core", 1, 2)
    p10, side, far = lax.optimization_barrier((p10, side, far))
    traces = [trace, far, side, shift(side, "core", 1, 2)]
    p11 = shift(p10, "core", 1, 2)

    def chol1(*refs):
        chol_kernel(1.0 / tokens, damping_ratio / (tokens * width), *refs)

    fac, fac_half = call(
        chol1,
        (shape((NP, NB, NB), bf16), shape((HALF, NB, NB), bf16)),
        "svvvvvvvv",
        "vv",
        [square, square, diag],
        "chol_gram",
    )(ids, p00, p01, p10, p11, *traces)
    sk_all = call(stage_kernel, shape(sk_all.shape, bf16), "a", "v", [pltpu.SemaphoreType.DMA], "stage")(sk_all)
    got = [shift(fac_half, "x", s, 4) for s in (1, 2, 3)]
    got_oth = [shift(v, "core", 1, 2) for v in got]
    pair_shape = shape((2, NP, NB, NB), bf16)
    unpacked = [pltpu.VMEM((2, WB, WB), bf16)]
    ypart, first = call(
        mixed_first_kernel, (shape((4 * n, WB)), pair_shape), "svvvvv", "vv", unpacked, "mixed_first"
    )(ids, fac, got[2], got_oth[2], sk_all, weight)
    ypart, second = call(
        mixed_kernel, (shape((4, n, WB), bf16), pair_shape), "s" + "v" * 7, "vv", unpacked, "mixed"
    )(ids, got[0], got_oth[0], got[1], got_oth[1], sk_all, weight, ypart)

    ypieces = lax.all_to_all(ypart, "col", 0, 0, tiled=True)
    tri = shape((16, HALF, 8, NB))
    cown, coth, ysum = call(cross_kernel, (tri, tri, shape((n, WB), bf16)), "sv", "vvv", [], "cross")(ids, ypieces)
    ys = [shift(ysum, "col", s, 4) for s in (1, 2, 3)]
    half = cown + shift(coth, "core", 1, 2)
    piece = jnp.sum(lax.all_to_all(half, ("x", "col"), 0, 0, tiled=True), axis=0)
    *ys, _ = lax.optimization_barrier(ys + [piece])

    parts = (4, WB, 256)
    toth, yb = call(
        send_kernel,
        (shape(parts, bf16), shape((4 * n, WB), bf16)),
        "svvvvv",
        "vv",
        [pltpu.VMEM((4 * n, WB), f32)],
        "moments_send",
        cost=brief,
    )(ids, ysum, *ys, weight)
    t = call(keep_kernel, shape(parts, bf16), "svvv", "v", [], "moments_keep", cost=brief)(
        ids, yb, weight, shift(toth, "core", 1, 2)
    )
    piece = jnp.sum(everyone(piece, "row", 8), axis=0)
    piece, t = lax.optimization_barrier((piece, t))
    t = lax.psum_scatter(t, "x", scatter_dimension=0, tiled=True)
    half = everyone(piece, ("x", "col"), 16)
    coth = shift(half, "core", 1, 2)

    def chol2(*refs):
        chol2_kernel(1.0 / hidden, *refs)

    inv = call(chol2, shape((WB, WB)), "svv", "v", [square, square, diag], "chol_cross")(ids, half, coth)
    parts = call(part_kernel, shape((64, 16, NB), bf16), "vv", "v", [], "project")(inv, t)
    parts = lax.all_to_all(parts, ("x", "core", "row"), 0, 0, tiled=True)

    def final(*refs):
        final_kernel(1.0 / math.sqrt(hidden), *refs)

    projections = call(final, shape((8, 4 * WB)), "svvv", "v", [pltpu.VMEM((8, 4 * WB), f32)], "final")(
        ids, parts, first, second
    )
    panels = call(panel_kernel, shape((4 * n, WB)), "vv", "v", [], "panels")(inv, yb)
    return (panels, projections)


def solution(mesh):
    fine = jax.sharding.Mesh(mesh.devices.reshape(4, 2, 8, 4), ("x", "core", "row", "col"))
    return jax.shard_map(
        shards,
        mesh=fine,
        in_specs=(P(("x", "core"), "col"), P(("x", "core", "row"), "col"), P("col", "row")),
        out_specs=(P(("x", "core", "row"), None), P(("x", "core", "row"), "col")),
        check_vma=False,
    )
```
